32 devices in a mesh: dp: 4 (over z), shard: 8 (over y, x, core).
Axes of the slice: x: 2, y: 2, z: 4, core: 2. Of those that a mesh axis runs over, the one named last changes fastest.
Arguments:
- prefill_x: bfloat16 [24576, 1536], P(('dp', 'shard')), may hold values from -6 to 6
- decode_x: bfloat16 [16, 1536], P('dp'), may hold values from -6 to 6
- norm_gain: bfloat16 [1536], P(('dp', 'shard')), may hold values from 0.099609375 to 1.8984375
- wqkv: bfloat16 [1536, 3072], P(('dp', 'shard')), may hold values from -0.15625 to 0.15625
- wo: bfloat16 [1536, 1536], P(('dp', 'shard')), may hold values from -0.15625 to 0.15625
- k_cache: bfloat16 [16, 4096, 768], P('dp', 'shard'), may hold values from -360 to 360
- v_cache: bfloat16 [16, 4096, 768], P('dp', 'shard'), may hold values from -6 to 6
- cache_len: int32 [16], P('dp'), may hold values from 1 to 4096, as said below
Outputs:
- prefill_out: bfloat16 [24576, 1536], P(('dp', 'shard'))
- decode_out: bfloat16 [16, 1536], P('dp')
The draws below stay inside these ranges and needn't reach their ends.
Inputs may be any that keep to these rules, and one draw needn't show every extreme that they name: `cache_len`: some request has exactly 4096 cached positions.
All inputs are finite; a program needn't handle non-finite values.
Results may differ from the reference program's by a relative error of at most 0.0095.
The reference program's roundings to bfloat16 on the way count: a program that leaves them out, or rounds other values in their place, can miss the bound.
Values may be sent and summed in bfloat16 or wider, within the bound.
No kernel may reach another device: no remote copies, remote signals or barrier semaphores. Data moves between devices by JAX's collectives and lax.ppermute only.
A program may use at most 128 MiB of HBM per device.

```python
import jax
import jax.numpy as jnp
from jax import lax

D = 1536
H = 16
KV = 8
HD = 96
STRETCH = 768
CL_DEV = 512
QKVW = 3072
CACHE = 4096
REQS = 16
TOKENS = 24576
N_SHARD = 8


def draw_k_cache(key, part):
    left_key = jax.random.fold_in(key, 0)
    drawn = jax.random.truncated_normal(left_key, -6.0, 6.0, (REQS, CACHE, KV * HD), jnp.float32) * 2.0
    return drawn.astype(jnp.bfloat16)


def draw_cache_len(key, part):
    left_key, right_key = jax.random.split(key)
    lengths = jax.random.randint(left_key, (REQS,), 1, CACHE + 1)
    chosen = jax.random.randint(right_key, (), 0, REQS)
    return jnp.where(jnp.arange(REQS) == chosen, CACHE, lengths).astype(jnp.int32)


def block_levels(key, dims, cuts, least, top_value):
    loudness, own = 1.0, jax.random.fold_in(key, 6)
    for position, shards_of in cuts:
        heights = jnp.exp(jax.random.uniform(jax.random.fold_in(own, position), (shards_of,), jnp.float32, least / len(cuts), top_value / len(cuts)))
        loudness = loudness * jnp.repeat(heights, dims[position] // shards_of).reshape([-1 if axis == position else 1 for axis in range(len(dims))])
    return loudness


def bell_draw(key, dims, spread, bound, cuts=(), kind=jnp.bfloat16):
    entries = spread * jax.random.normal(key, dims, jnp.float32)
    if cuts:
        entries = entries * block_levels(key, dims, cuts, -0.22, 0.18)
    return jnp.clip(entries, -bound, bound).astype(kind)


def setup_inputs(seed: int = 0) -> dict:
    keys = jax.random.split(jax.random.key(seed), 9)
    prefill_x = bell_draw(keys[0], (TOKENS, D), 1.0, 6.0, ((0, 32),))
    decode_x = bell_draw(keys[1], (REQS, D), 1.0, 6.0, ((0, 4),))
    norm_gain = jnp.clip(1.0 + 0.18 * jax.random.normal(keys[2], (D,), jnp.float32), 0.099609375, 1.8984375).astype(jnp.bfloat16)
    wqkv = bell_draw(keys[3], (D, QKVW), D ** -0.5, 0.15625, ((0, 32),))
    wo = bell_draw(keys[4], (D, D), D ** -0.5, 0.15625, ((0, 32),))
    k_cache = draw_k_cache(jax.random.fold_in(keys[8], 71), 0)
    v_cache = bell_draw(keys[6], (REQS, CACHE, KV * HD), 1.0, 6.0, ((0, 4), (1, 8)))
    cache_len = draw_cache_len(jax.random.fold_in(keys[8], 71), 0)
    return {"prefill_x": prefill_x, "decode_x": decode_x, "norm_gain": norm_gain, "wqkv": wqkv, "wo": wo, "k_cache": k_cache, "v_cache": v_cache, "cache_len": cache_len}


THETA = 100000.0
EPS = 1e-05
NEGATIVE = -1e+30

def normalize(inputs, norm_gain):
    widened = inputs.astype(jnp.float32)
    factor = lax.rsqrt(lax.optimization_barrier(jnp.mean(widened * widened, axis=-1, keepdims=True)) + EPS)
    return (widened * factor * norm_gain.astype(jnp.float32)).astype(jnp.bfloat16)

def rotate(tensor, positions):
    half_width = tensor.shape[-1] // 2
    frequency = jnp.power(THETA, -jnp.arange(half_width, dtype=jnp.float32) * (2.0 / tensor.shape[-1]))
    angles = positions.astype(jnp.float32)[:, None] * frequency[None, :]
    cosine = jnp.cos(angles)[:, None, :]
    sine_part = jnp.sin(angles)[:, None, :]
    leading = tensor[..., :half_width]
    trailing = tensor[..., half_width:]
    return jnp.concatenate([leading * cosine - trailing * sine_part, trailing * cosine + leading * sine_part], axis=-1)

def project_heads(normed, wqkv, positions):
    united_rows = jnp.dot(normed, wqkv, preferred_element_type=jnp.float32)
    row_count = united_rows.shape[0]
    queries = rotate(united_rows[:, :H * HD].reshape(row_count, H, HD), positions).astype(jnp.bfloat16)
    new_keys = rotate(united_rows[:, H * HD:(H + KV) * HD].reshape(row_count, KV, HD), positions).astype(jnp.bfloat16)
    new_values = united_rows[:, (H + KV) * HD:].reshape(row_count, KV, HD).astype(jnp.bfloat16)
    return (queries, new_keys, new_values)

def causal_stretch(queries, new_keys, new_values):
    row_count = queries.shape[0]
    group_size = H // KV
    query_heads = jnp.moveaxis(queries.reshape(row_count, KV, group_size, HD), 1, 0)
    key_heads = jnp.moveaxis(new_keys, 1, 0)
    value_heads = jnp.moveaxis(new_values, 1, 0)
    indices = jnp.arange(row_count, dtype=jnp.int32)
    allowed = indices[None, :] <= indices[:, None]

    def one_head(operands):
        query_head, key_head, value_head = operands
        scores = jnp.einsum('qgd,sd->gqs', query_head.astype(jnp.float32), key_head.astype(jnp.float32)) * HD ** (-0.5)
        scores = jnp.where(allowed[None], scores, NEGATIVE)
        highest = lax.optimization_barrier(jnp.max(scores, axis=-1, keepdims=True))
        expanded = jnp.exp(scores - highest)
        weights = (expanded / lax.optimization_barrier(jnp.sum(expanded, axis=-1, keepdims=True))).astype(jnp.bfloat16)
        weights = lax.optimization_barrier(weights)
        return jnp.einsum('gqs,sd->qgd', weights.astype(jnp.float32), value_head.astype(jnp.float32)).astype(jnp.bfloat16)
    attended = lax.map(one_head, (query_heads, key_heads, value_heads))
    return jnp.moveaxis(attended, 0, 1).reshape(row_count, H * HD)

def decode_one(operands):
    queries, self_key, self_value, cache_keys, cache_values, length = operands
    group_size = H // KV
    score_scale = HD ** (-0.5)
    query_heads = queries.reshape(KV, group_size, HD).astype(jnp.float32)
    key_blocks = cache_keys.reshape(N_SHARD, CL_DEV, KV, HD).astype(jnp.float32)
    value_blocks = cache_values.reshape(N_SHARD, CL_DEV, KV, HD).astype(jnp.float32)
    scores = jnp.einsum('kgd,bpkd->bkgp', query_heads, key_blocks) * score_scale
    positions = jnp.arange(N_SHARD * CL_DEV, dtype=jnp.int32).reshape(N_SHARD, 1, 1, CL_DEV)
    live_mask = positions < length
    scores = jnp.where(live_mask, scores, NEGATIVE)
    block_peaks = lax.optimization_barrier(jnp.max(scores, axis=-1))
    expanded = jnp.where(live_mask, jnp.exp(scores - block_peaks[..., None]), 0.0)
    partial_totals = lax.optimization_barrier(jnp.sum(expanded, axis=-1))
    rounded = lax.optimization_barrier(expanded.astype(jnp.bfloat16))
    partial_sums = jnp.einsum('bkgp,bpkd->bkgd', rounded.astype(jnp.float32), value_blocks)
    self_scores = jnp.einsum('kgd,kd->kg', query_heads, self_key.astype(jnp.float32)) * score_scale
    overall = jnp.maximum(lax.optimization_barrier(jnp.max(block_peaks, axis=0)), self_scores)
    rescale = jnp.exp(block_peaks - overall[None])
    own_weight = jnp.exp(self_scores - overall)
    numerator = lax.optimization_barrier(jnp.sum(partial_sums * rescale[..., None], axis=0)) + own_weight[..., None] * self_value.astype(jnp.float32)[:, None, :]
    denominator = lax.optimization_barrier(jnp.sum(partial_totals * rescale, axis=0)) + own_weight
    return (numerator / denominator[..., None]).reshape(H * HD).astype(jnp.bfloat16)

def reference(prefill_x, decode_x, norm_gain, wqkv, wo, k_cache, v_cache, cache_len):
    stretched = prefill_x.reshape(TOKENS // STRETCH, STRETCH, D)

    def one_stretch(inputs):
        normed = normalize(inputs, norm_gain)
        queries, new_keys, new_values = project_heads(normed, wqkv, jnp.arange(STRETCH, dtype=jnp.int32))
        attended = causal_stretch(queries, new_keys, new_values)
        return jnp.dot(attended, wo, preferred_element_type=jnp.float32).astype(jnp.bfloat16)
    prefill_out = lax.map(one_stretch, stretched).reshape(TOKENS, D)
    normed = normalize(decode_x, norm_gain)
    queries, new_keys, new_values = project_heads(normed, wqkv, cache_len)
    attended = lax.map(decode_one, (queries, new_keys, new_values, k_cache, v_cache, cache_len))
    decode_out = jnp.dot(attended, wo, preferred_element_type=jnp.float32).astype(jnp.bfloat16)
    return (prefill_out, decode_out)
```

```python
import functools

import jax
import jax.numpy as jnp
from jax import lax
from jax.experimental import pallas as pl
from jax.experimental.pallas import tpu as pltpu
from jax.sharding import PartitionSpec as P

H = 16
KV = 8
HD = 96
HALF = HD // 2
LANES = 128
PAD = H * LANES

THETA = 100000.0
EPS = 1e-05
NEGATIVE = -1e30
SCALE = HD ** (-0.5)
LOG2E = 1.4426950408889634

BF16 = jnp.bfloat16
F32 = jnp.float32
VMEM_BYTES = 56 * 1024 * 1024


def rope_tables(positions, width):
    lane = jnp.arange(width, dtype=jnp.int32)
    lane = lane % HD if width % HD == 0 else lane
    frequency = jnp.power(THETA, -(lane % HALF).astype(F32) * (2.0 / HD))
    angles = positions.astype(F32)[:, None] * frequency[None, :]
    cosine, sine = jnp.cos(angles), jnp.sin(angles)
    lane = lane[None, :]
    return jnp.stack(
        [
            jnp.where(lane < HD, cosine, 0.0),
            jnp.where((lane >= HALF) & (lane < HD), sine, 0.0),
            jnp.where(lane < HALF, -sine, 0.0),
        ]
    )


def normalize(rows, gain):
    widened = rows.astype(F32)
    factor = lax.rsqrt(jnp.mean(widened * widened, axis=-1, keepdims=True) + EPS)
    return (widened * factor * gain).astype(BF16)


def project_kernel(block_rows, plan, rope, offs_ref, *rest):
    count = 1 + max(source[0] for sources in plan for source in sources)
    w_refs, rest = rest[:count], rest[count:]
    if rope:
        xn_ref, table_ref, dtable_ref, heads_ref, dec_ref, w_ref, *u_refs, w_sem = rest
    else:
        x_ref, sib_ref, dx_ref, table_ref, dtable_ref, heads_ref, dec_ref, xn_ref, w_ref, *u_refs, gain_ref, w_sem = rest
    half = KV * HD // 2
    width = 2 * half
    rows_all = xn_ref.shape[0]
    main = heads_ref.shape[1]
    stretch = main // 2

    for t, sources in enumerate(plan):
        for ref, column, first, blocks in sources:
            for b in range(blocks):
                rows = pl.ds(pl.multiple_of(offs_ref[first + b], 16), block_rows)
                pltpu.make_async_copy(
                    w_refs[ref].at[pl.ds(b * block_rows, block_rows), pl.ds(column, half if t < 2 else LANES)],
                    w_ref.at[rows, pl.ds(t * half, half)] if t < 2 else gain_ref.at[rows],
                    w_sem.at[t // 2],
                ).start()

    if not rope:
        pltpu.make_async_copy(gain_ref, gain_ref, w_sem.at[1]).wait()
        pick = (lax.broadcasted_iota(jnp.int32, (8, LANES), 1) == 0).astype(BF16)
        gain = lax.dot_general(pick, gain_ref[...], (((1,), (1,)), ((), ())), preferred_element_type=F32)[0:1]

        def body(i, _):
            rows = pl.ds(pl.multiple_of(i * 64, 64), 64)
            xn_ref[rows, :] = normalize(x_ref[rows, :], gain)
            xn_ref[pl.ds(pl.multiple_of(i * 64 + stretch, 64), 64), :] = normalize(sib_ref[rows, :], gain)
            return 0

        lax.fori_loop(0, stretch // 64, body, 0)
        xn_ref[main:, :] = normalize(dx_ref[...], gain)

    pltpu.make_async_copy(w_ref, w_ref, w_sem.at[0]).wait()

    chunk = 256
    lane = lax.broadcasted_iota(jnp.int32, (chunk, LANES), 1)
    for i in range(main // chunk):
        u_ref = u_refs[i % 2]
        first, last = i * chunk, (i + 1) * chunk
        whole = slice(first, last if last < main else rows_all)
        for n in range(width // 256):
            u_ref[: whole.stop - first, n * 256 : (n + 1) * 256] = jnp.dot(
                xn_ref[whole, :], w_ref[:, n * 256 : (n + 1) * 256], preferred_element_type=F32
            )
        at = slice(first % stretch, first % stretch + chunk)
        for h in range(8):
            u = head_tile(u_ref, slice(0, chunk), h)
            if rope or h < 4:
                u = (
                    u * table_ref[0, at, :]
                    + pltpu.roll(u, HALF, 1) * table_ref[1, at, :]
                    + pltpu.roll(u, LANES - HALF, 1) * table_ref[2, at, :]
                )
            else:
                u = jnp.where(lane < HD, u, 1.0)
            heads_ref[h, first:last, :] = u.astype(BF16)
        if last == main:
            u = u_ref[chunk : chunk + rows_all - main, :]
            turned = (
                u * dtable_ref[0]
                + pltpu.roll(u, HALF, 1) * dtable_ref[1]
                + pltpu.roll(u, width - HALF, 1) * dtable_ref[2]
            )
            dec_ref[...] = turned.astype(BF16)


def project(rope, operands, tables, dtable, offs, w_pieces, block_rows, plan):
    depth = operands[0].shape[1]
    rows_all = sum(operand.shape[0] for operand in operands)
    width = KV * HD
    extra = dtable.shape[1]
    main = rows_all - extra
    smem = pl.BlockSpec(memory_space=pltpu.SMEM)
    vmem = pl.BlockSpec(memory_space=pltpu.VMEM)
    hbm = pl.BlockSpec(memory_space=pl.ANY)
    out_shape = [
        jax.ShapeDtypeStruct((8, main, LANES), BF16),
        jax.ShapeDtypeStruct((extra, width), BF16),
    ]
    scratch = [pltpu.VMEM((depth, width), BF16)] + [pltpu.VMEM((256 + extra, width), F32)] * 2
    if not rope:
        out_shape.append(jax.ShapeDtypeStruct((rows_all, depth), BF16))
        scratch.append(pltpu.VMEM((depth, LANES), BF16))
    return pl.pallas_call(
        functools.partial(project_kernel, block_rows, plan, rope),
        in_specs=[smem] + [hbm] * len(w_pieces) + [vmem] * (len(operands) + 2),
        out_specs=[vmem] * len(out_shape),
        out_shape=out_shape,
        scratch_shapes=scratch + [pltpu.SemaphoreType.DMA((2,))],
        compiler_params=pltpu.CompilerParams(vmem_limit_bytes=VMEM_BYTES),
        cost_estimate=pl.CostEstimate(
            flops=2 * rows_all * depth * width, bytes_accessed=12_000_000, transcendentals=0
        ),
        name="project_q" if rope else "project_kv",
    )(offs, *w_pieces, *operands, tables, dtable)


def head_tile(u_ref, rows, index):
    base, place = (index // 4) * 3 * LANES, index % 4
    lane = lax.broadcasted_iota(jnp.int32, (rows.stop - rows.start, LANES), 1)

    def tile(t):
        return u_ref[rows, base + t * LANES : base + (t + 1) * LANES]

    if place == 0:
        return tile(0)
    if place == 1:
        return pltpu.roll(jnp.where(lane >= 96, tile(0), tile(1)), 32, 1)
    if place == 2:
        return pltpu.roll(jnp.where(lane >= 64, tile(1), tile(2)), 64, 1)
    return pltpu.roll(tile(2), 96, 1)


def decode_kernel(core_ref, len_ref, start_ref, mine_ref, other_ref, k_ref, v_ref, part_ref, self_ref, query_ref):
    step = pl.program_id(0)
    requests, span, width = pl.num_programs(0), k_ref.shape[1], k_ref.shape[2]
    half = width // 2
    count = self_ref.shape[1] // 2

    @pl.when(step == 0)
    def _():
        mine, other = mine_ref[...].astype(F32), other_ref[...].astype(F32)
        mine_first = core_ref[0] == 0
        low, high = jnp.where(mine_first, mine, other), jnp.where(mine_first, other, mine)
        own_k = jnp.concatenate([low[:, width : width + half], high[:, width : width + half]], axis=1)
        own_v = jnp.concatenate([low[:, width + half :], high[:, width + half :]], axis=1)
        at_lane = lax.broadcasted_iota(jnp.int32, own_k.shape, 1) // HD
        for parity in range(2):
            query = jnp.concatenate(
                [side[:, h * HD : (h + 1) * HD] for side in (low, high) for h in range(parity, 8, 2)], axis=1
            )
            query_ref[parity] = query
            product = query * own_k
            own = jnp.zeros(own_k.shape, F32)
            for j in range(KV):
                here = at_lane == j
                own = own + jnp.where(
                    here, jnp.sum(jnp.where(here, product, 0.0), axis=-1, keepdims=True), 0.0
                )
            self_ref[0, parity * count : (parity + 1) * count, :] = own[:count] * SCALE
            self_ref[1, parity * count : (parity + 1) * count, :] = own_v[:count]

    diagonal = (
        lax.broadcasted_iota(jnp.int32, (KV, width), 1) // HD
        == lax.broadcasted_iota(jnp.int32, (KV, width), 0)
    )
    query = jnp.concatenate(
        [
            jnp.where(diagonal, jnp.broadcast_to(query_ref[p, pl.ds(step, 1), :], (KV, width)), 0.0)
            for p in range(2)
        ],
        axis=0,
    ).astype(BF16)
    scores = (
        lax.dot_general(query, k_ref[0], (((1,), (1,)), ((), ())), preferred_element_type=F32) * SCALE
    )
    live = lax.broadcasted_iota(jnp.int32, (H, span), 1) + start_ref[0] < len_ref[step]
    scores = jnp.where(live, scores, NEGATIVE)
    peak = jnp.max(scores, axis=-1, keepdims=True)
    expanded = jnp.where(live, jnp.exp(scores - peak), 0.0)
    total = jnp.sum(expanded, axis=-1, keepdims=True)
    sums = jnp.dot(expanded.astype(BF16), v_ref[0], preferred_element_type=F32)
    for slot, values in enumerate((sums, peak, total)):
        for parity in range(2):
            part_ref[slot, pl.ds(parity * requests + step, 1), :] = jnp.sum(
                jnp.where(diagonal, values[parity * KV : (parity + 1) * KV], 0.0), axis=0, keepdims=True
            )


def decode(core, cache_len, start, mine, other, k_cache, v_cache):
    requests, span, width = k_cache.shape
    smem = pl.BlockSpec(memory_space=pltpu.SMEM)
    vmem = pl.BlockSpec(memory_space=pltpu.VMEM)
    block = pl.BlockSpec((1, span, width), lambda r: (r, 0, 0))
    return pl.pallas_call(
        decode_kernel,
        grid=(requests,),
        in_specs=[smem] * 3 + [vmem] * 2 + [block] * 2,
        out_specs=[vmem] * 2,
        out_shape=[
            jax.ShapeDtypeStruct((3, 2 * requests, width), F32),
            jax.ShapeDtypeStruct((2, 2 * requests, width), F32),
        ],
        scratch_shapes=[pltpu.VMEM((2, mine.shape[0], width), F32)],
        compiler_params=pltpu.CompilerParams(
            dimension_semantics=("arbitrary",), vmem_limit_bytes=VMEM_BYTES
        ),
        cost_estimate=pl.CostEstimate(
            flops=2_000_000_000, bytes_accessed=2 * requests * span * width * 2, transcendentals=0
        ),
        name="decode",
    )(core, cache_len, start, mine, other, k_cache, v_cache)


def attend_kernel(block, q_ref, k_ref, v_ref, o_ref):
    stretch = o_ref.shape[0]
    causal = lax.broadcasted_iota(jnp.int32, (block, block), 1) <= lax.broadcasted_iota(
        jnp.int32, (block, block), 0
    )
    for parity in range(2):
        for i in range(stretch // block):
            rows = slice(i * block, (i + 1) * block)
            seen = (i + 1) * block
            scores = lax.dot_general(
                q_ref[parity, rows, :], k_ref[0, :seen, :], (((1,), (1,)), ((), ())),
                preferred_element_type=F32,
            )
            last = jnp.where(causal, scores[:, i * block :], NEGATIVE)
            scores = last if i == 0 else jnp.concatenate([scores[:, : i * block], last], axis=1)
            peak = jnp.max(scores, axis=-1, keepdims=True)
            weights = jnp.exp2((scores - peak) * (SCALE * LOG2E)).astype(BF16)
            mixed = jnp.dot(weights, v_ref[0, :seen, :], preferred_element_type=F32)
            o_ref[rows, parity * LANES : (parity + 1) * LANES] = (mixed / mixed[:, HD : HD + 1]).astype(BF16)


def attend(queries, keys_values, which):
    stretch = queries.shape[1] // 2
    return pl.pallas_call(
        functools.partial(attend_kernel, 256),
        grid=(KV // 2,),
        in_specs=[
            pl.BlockSpec((2, stretch, LANES), lambda j: (j, which, 0)),
            pl.BlockSpec((1, stretch, LANES), lambda j: (j, which, 0)),
            pl.BlockSpec((1, stretch, LANES), lambda j: (KV // 2 + j, which, 0)),
        ],
        out_specs=pl.BlockSpec((stretch, 2 * LANES), lambda j: (0, j)),
        out_shape=jax.ShapeDtypeStruct((stretch, PAD // 2), BF16),
        compiler_params=pltpu.CompilerParams(
            dimension_semantics=("arbitrary",), vmem_limit_bytes=VMEM_BYTES
        ),
        cost_estimate=pl.CostEstimate(
            flops=10_000_000_000, bytes_accessed=5_000_000, transcendentals=H // 2 * stretch * stretch
        ),
        name="attend",
    )(queries, keys_values, keys_values)


def output_kernel(requests, core_ref, wo_hbm, mine_hbm, other_hbm, part_ref, self_ref, out_ref, dec_ref, wo_ref, att_ref, w_sem, o_sem):
    step = pl.program_id(0)
    stretch = out_ref.shape[0]
    columns = out_ref.shape[1]
    steps = wo_ref.shape[0]
    half = PAD // 2

    @pl.when(step == 0)
    def _():
        core = core_ref[0]
        o_copies = [
            pltpu.make_async_copy(source, att_ref.at[place, pl.ds(0, stretch)], o_sem.at[n])
            for n, (source, place) in enumerate(((mine_hbm, core), (other_hbm, 1 - core)))
        ]
        for copy in o_copies:
            copy.start()
        for t in range(steps):
            for h in range(H):
                pltpu.make_async_copy(
                    wo_hbm.at[pl.ds(h * HD, HD), pl.ds(t * columns, columns)],
                    wo_ref.at[t, pl.ds(h * LANES, HD)],
                    w_sem.at[t],
                ).start()
        for t in range(steps):
            for h in range(H):
                wo_ref[t, h * LANES + HD : (h + 1) * LANES, :] = jnp.zeros((LANES - HD, columns), BF16)
        own, own_v = self_ref[0], self_ref[1]
        peak = part_ref[1]
        top = jnp.maximum(own, peak)
        rescale, own_weight = jnp.exp(peak - top), jnp.exp(own - top)
        mix = (part_ref[0] * rescale + own_weight * own_v) / (part_ref[2] * rescale + own_weight)
        extra = att_ref.shape[1] - stretch
        att_ref[:, stretch:, :] = jnp.zeros((2, extra, half), BF16)
        for parity in range(2):
            mine = mix[parity * requests : (parity + 1) * requests]
            mine = jnp.concatenate([mine, jnp.zeros((extra - requests, mine.shape[1]), F32)], axis=0)
            for j in range(KV):
                h = 2 * j + parity
                at = h % 8 * LANES
                att_ref[h // 8, stretch:, at : at + HD] = mine[:, j * HD : (j + 1) * HD].astype(BF16)
        for copy in o_copies:
            copy.wait()

    for t in range(steps):
        @pl.when(step == t)
        def _():
            whole = wo_ref.at[t, pl.ds(0, H * HD)]
            pltpu.make_async_copy(whole, whole, w_sem.at[t]).wait()

    projected = jnp.dot(att_ref[0], wo_ref[step, :half], preferred_element_type=F32) + jnp.dot(
        att_ref[1], wo_ref[step, half:], preferred_element_type=F32
    )
    out_ref[...] = projected[:stretch].astype(BF16)
    dec_ref[...] = projected[stretch : stretch + requests].astype(BF16)


def output(mine, other, part, own, core, wo_all, requests):
    stretch = mine.shape[0]
    width = wo_all.shape[1]
    steps, extra = 3, 16
    smem = pl.BlockSpec(memory_space=pltpu.SMEM)
    vmem = pl.BlockSpec(memory_space=pltpu.VMEM)
    hbm = pl.BlockSpec(memory_space=pl.ANY)
    return pl.pallas_call(
        functools.partial(output_kernel, requests),
        grid=(steps,),
        in_specs=[smem] + [hbm] * 3 + [vmem] * 2,
        out_specs=[
            pl.BlockSpec((stretch, width // steps), lambda t: (0, t)),
            pl.BlockSpec((requests, width // steps), lambda t: (0, t)),
        ],
        out_shape=[
            jax.ShapeDtypeStruct((stretch, width), BF16),
            jax.ShapeDtypeStruct((requests, width), BF16),
        ],
        scratch_shapes=[
            pltpu.VMEM((steps, PAD, width // steps), BF16),
            pltpu.VMEM((2, stretch + extra, PAD // 2), BF16),
            pltpu.SemaphoreType.DMA((steps,)),
            pltpu.SemaphoreType.DMA((2,)),
        ],
        compiler_params=pltpu.CompilerParams(
            dimension_semantics=("arbitrary",), vmem_limit_bytes=VMEM_BYTES
        ),
        cost_estimate=pl.CostEstimate(
            flops=2 * stretch * PAD * width, bytes_accessed=12_000_000, transcendentals=0
        ),
        name="output",
    )(core, wo_all, mine, other, part, own)


def swap(array, mask, n_shard):
    return lax.ppermute(array, "shard", [(i, i ^ mask) for i in range(n_shard)])


def spread(local, cut, n_dp, n_shard):
    along = [local]
    for shift in range(1, n_dp):
        along.append(lax.ppermute(local, "dp", [((i + shift) % n_dp, i) for i in range(n_dp)]))
    here = jnp.concatenate(along, axis=0)
    whole = local.shape[1]
    beside, above = swap(here, 2, n_shard), swap(here, 4, n_shard)
    left, right = swap(beside[:, :cut], 4, n_shard), swap(above[:, cut:], 2, n_shard)
    return [(here, 0, 0, whole), (beside, 1, 0, whole), (above, 2, 0, whole), (left, 3, 0, cut), (right, 3, cut, whole)]


def merge(first, second):
    top = jnp.maximum(first[1], second[1])
    one, two = jnp.exp(first[1] - top), jnp.exp(second[1] - top)
    return jnp.stack([first[0] * one + second[0] * two, top, first[2] * one + second[2] * two])


def per_device(n_dp, n_shard, prefill_x, decode_x, norm_gain, wqkv, wo, k_cache, v_cache, cache_len):
    stretch = prefill_x.shape[0]
    requests, span, width = k_cache.shape
    half = width // 2
    me, me_dp = lax.axis_index("shard"), lax.axis_index("dp")
    core = me % 2
    everyone = ("dp", "shard")
    block_rows = wqkv.shape[0]
    low = [wqkv[:, 2 * width : 2 * width + half], wqkv[:, 3 * width : 3 * width + half], wqkv[:, :width]]
    high = [wqkv[:, 2 * width + half : 3 * width], wqkv[:, 3 * width + half :], wqkv[:, width : 2 * width]]
    low, high = jnp.concatenate(low, axis=1), jnp.concatenate(high, axis=1)
    gain_columns = jnp.broadcast_to(norm_gain[:, None], (block_rows, LANES))
    head = LANES + width
    split = n_shard == 8 and block_rows == HALF

    wo_all = lax.all_gather(wo, everyone, axis=0, tiled=True)
    sib_x = swap(prefill_x, 1, n_shard)
    kv_plan, q_plan = [[], [], []], [[], []]
    if split:
        first = core == 0
        mine = jnp.concatenate([gain_columns, jnp.where(first, low, high)], axis=1)
        theirs = jnp.concatenate([gain_columns, jnp.where(first, high, low)], axis=1)
        theirs = swap(theirs, 1, n_shard)
        pair = jnp.concatenate([jnp.where(first, mine, theirs), jnp.where(first, theirs, mine)], axis=0)
        order = jnp.arange(n_shard // 2 * n_dp, dtype=jnp.int32)
        chip = (me_dp + order % n_dp) % n_dp * (n_shard // 2) + (me // 2 ^ (order // n_dp))
        block_rows = 2 * block_rows
        offs = chip * block_rows
        kv_pieces = spread(pair[:, :head], LANES + half, n_dp, n_shard)
        later, _ = lax.optimization_barrier((pair[:, head:], kv_pieces[0][0]))
        q_pieces = spread(later, half, n_dp, n_shard)
        for pieces, plan, starts in (
            (kv_pieces, kv_plan, {LANES: 0, LANES + half: 1, 0: 2}),
            (q_pieces, q_plan, {0: 0, half: 1}),
        ):
            for index, (_, mask, left, right) in enumerate(pieces):
                for column, t in starts.items():
                    if left <= column < right:
                        plan[t].append((index, column - left, mask * n_dp, n_dp))
        kv_pieces, q_pieces = [piece[0] for piece in kv_pieces], [piece[0] for piece in q_pieces]
    else:
        offs = jnp.zeros((1,), jnp.int32)
        every = lax.all_gather(jnp.concatenate([gain_columns, low, high], axis=1), everyone, axis=0, tiled=True)
        block_rows = every.shape[0]
        chosen = jnp.where(core == 0, every[:, LANES : LANES + 2 * width], every[:, LANES + 2 * width :])
        kv_pieces = [jnp.concatenate([every[:, :LANES], chosen[:, :width]], axis=1)]
        q_pieces = [chosen[:, width:]]
        kv_plan = [[(0, LANES, 0, 1)], [(0, LANES + half, 0, 1)], [(0, 0, 0, 1)]]
        q_plan = [[(0, 0, 0, 1)], [(0, half, 0, 1)]]

    extra = 16
    dx = jnp.pad(decode_x, ((0, extra - requests), (0, 0)))
    decode_positions = jnp.concatenate([cache_len, jnp.zeros((extra - requests,), jnp.int32)])
    tables = rope_tables(jnp.arange(stretch, dtype=jnp.int32), LANES)
    q_table = rope_tables(decode_positions, width)
    plain = jnp.stack([jnp.ones((extra, half), F32)] + [jnp.zeros((extra, half), F32)] * 2)
    kv_table = jnp.concatenate([q_table[:, :, :half], plain], axis=2)
    keys_values, dec_kv, xn = project(
        False, [prefill_x, sib_x, dx], tables, kv_table, offs, kv_pieces, block_rows, kv_plan
    )
    queries, dec_q = project(True, [xn], tables, q_table, offs, q_pieces, block_rows, q_plan)
    dec = jnp.concatenate([dec_q, dec_kv], axis=1)
    dec_other = swap(dec, 1, n_shard)
    core = core.astype(jnp.int32).reshape(1)
    theirs = attend(queries, keys_values, 1)
    other = swap(theirs, 1, n_shard)
    part, own = decode(core, cache_len, (me * span).reshape(1), dec, dec_other, k_cache, v_cache)
    mask = 1
    while mask < n_shard:
        received = swap(part, mask, n_shard)
        lower = (me & mask) == 0
        part = merge(jnp.where(lower, part, received), jnp.where(lower, received, part))
        mask *= 2
    mine = attend(queries, keys_values, 0)
    return output(mine, other, part, own, core, wo_all, requests)


def solution(mesh):
    in_specs = (
        P(("dp", "shard"), None),
        P("dp", None),
        P(("dp", "shard")),
        P(("dp", "shard"), None),
        P(("dp", "shard"), None),
        P("dp", "shard", None),
        P("dp", "shard", None),
        P("dp"),
    )
    out_specs = (P(("dp", "shard"), None), P("dp", None))
    return jax.shard_map(
        functools.partial(per_device, mesh.shape["dp"], mesh.shape["shard"]),
        mesh=mesh, in_specs=in_specs, out_specs=out_specs, check_vma=False,
    )
```

```python
import functools

import jax
import jax.numpy as jnp
from jax import lax
from jax.experimental import pallas as pl
from jax.experimental.pallas import tpu as pltpu
from jax.sharding import PartitionSpec as P

H = 16
KV = 8
HD = 96
HALF = HD // 2
LANES = 128
PAD = H * LANES

THETA = 100000.0
EPS = 1e-05
NEGATIVE = -1e30
SCALE = HD ** (-0.5)
LOG2E = 1.4426950408889634

BF16 = jnp.bfloat16
F32 = jnp.float32
VMEM_BYTES = 56 * 1024 * 1024


def cost(microseconds):
    return pl.CostEstimate(flops=int(microseconds * 1.1e9), bytes_accessed=100_000, transcendentals=0)


def rope_tables(positions, width):
    lane = jnp.arange(width, dtype=jnp.int32)
    lane = lane % HD if width % HD == 0 else lane
    frequency = jnp.power(THETA, -(lane % HALF).astype(F32) * (2.0 / HD))
    angles = positions.astype(F32)[:, None] * frequency[None, :]
    cosine, sine = jnp.cos(angles), jnp.sin(angles)
    lane = lane[None, :]
    return jnp.stack(
        [
            jnp.where(lane < HD, cosine, 0.0),
            jnp.where((lane >= HALF) & (lane < HD), sine, 0.0),
            jnp.where(lane < HALF, -sine, 0.0),
        ]
    )


def normalize(rows, gain):
    widened = rows.astype(F32)
    factor = lax.rsqrt(jnp.mean(widened * widened, axis=-1, keepdims=True) + EPS)
    return (widened * factor * gain).astype(BF16)


def head_tile(u_ref, rows, index):
    base, place = (index // 4) * 3 * LANES, index % 4
    lane = lax.broadcasted_iota(jnp.int32, (rows.stop - rows.start, LANES), 1)

    def tile(t):
        return u_ref[rows, base + t * LANES : base + (t + 1) * LANES]

    if place == 0:
        return tile(0)
    if place == 1:
        return pltpu.roll(jnp.where(lane >= 96, tile(0), tile(1)), 32, 1)
    if place == 2:
        return pltpu.roll(jnp.where(lane >= 64, tile(1), tile(2)), 64, 1)
    return pltpu.roll(tile(2), 96, 1)


def fetch(sources, refs, offs_ref, block_rows, columns, target, sem):
    for ref, column, first, blocks in sources:
        for b in range(blocks):
            to = pl.ds(pl.multiple_of(offs_ref[first + b], 16), block_rows)
            source = refs[ref].at[pl.ds(b * block_rows, block_rows), pl.ds(column, columns)]
            pltpu.make_async_copy(source, target(to), sem).start()


def fetch_weights(plan, refs, offs_ref, block_rows, w_ref, sem):
    half = w_ref.shape[1] // len(plan)
    for t, sources in enumerate(plan):
        fetch(sources, refs, offs_ref, block_rows, half, lambda rows: w_ref.at[rows, pl.ds(t * half, half)], sem)


def multiply(x, w_ref, u_ref, rows):
    for n in range(w_ref.shape[1] // 256):
        cols = slice(n * 256, (n + 1) * 256)
        u_ref[:rows, cols] = jnp.dot(x, w_ref[:, cols], preferred_element_type=F32)


def store_heads(u_ref, table_ref, heads_ref, first):
    rows = table_ref.shape[1]
    lane = lax.broadcasted_iota(jnp.int32, (rows, LANES), 1)
    for h in range(8):
        u = head_tile(u_ref, slice(0, rows), h)
        if h in (2, 3):
            u = jnp.where(lane < HD, u, 1.0)
        else:
            u = (
                u * table_ref[0]
                + pltpu.roll(u, HALF, 1) * table_ref[1]
                + pltpu.roll(u, LANES - HALF, 1) * table_ref[2]
            )
        heads_ref[h, first : first + rows, :] = u.astype(BF16)


def turn_decode(u, dtable_ref):
    return (
        u * dtable_ref[0]
        + pltpu.roll(u, HALF, 1) * dtable_ref[1]
        + pltpu.roll(u, u.shape[1] - HALF, 1) * dtable_ref[2]
    ).astype(BF16)


def attend(heads_ref, o_ref, block):
    stretch = o_ref.shape[0]
    causal = lax.broadcasted_iota(jnp.int32, (block, block), 1) <= lax.broadcasted_iota(
        jnp.int32, (block, block), 0
    )
    causal = jnp.concatenate([causal, causal], axis=0)
    for j in range(2):
        for i in range(stretch // block):
            rows = slice(i * block, (i + 1) * block)
            seen = (i + 1) * block
            both = heads_ref[4 + 2 * j : 6 + 2 * j, rows, :].reshape(2 * block, LANES)
            scores = lax.dot_general(
                both, heads_ref[j, :seen, :], (((1,), (1,)), ((), ())), preferred_element_type=F32
            )
            last = jnp.where(causal, scores[:, i * block :], NEGATIVE)
            scores = last if i == 0 else jnp.concatenate([scores[:, : i * block], last], axis=1)
            peak = jnp.max(scores, axis=-1, keepdims=True)
            weights = jnp.exp2((scores - peak) * (SCALE * LOG2E)).astype(BF16)
            mixed = jnp.dot(weights, heads_ref[2 + j, :seen, :], preferred_element_type=F32)
            mixed = (mixed / mixed[:, HD : HD + 1]).astype(BF16)
            for parity in range(2):
                lanes = slice((2 * j + parity) * LANES, (2 * j + parity + 1) * LANES)
                o_ref[rows, lanes] = mixed[parity * block : (parity + 1) * block]


def decode(turned, requests, offset, k_ref, v_ref, len_ref, start_ref, part_ref):
    turned = turned.astype(F32)
    extra = turned.shape[0]
    window, span = k_ref.shape[3], k_ref.shape[2]
    two = 2 * HD

    def widen(values):
        sides = [jnp.zeros((extra, offset), F32)] if offset else []
        sides += [values]
        sides += [jnp.zeros((extra, window - two - offset), F32)] if window - two - offset else []
        return jnp.concatenate(sides, axis=1)

    own_k, own_v = widen(turned[:, :two]), widen(turned[:, two : 2 * two])
    queries = []
    for parity in range(2):
        at = 2 * two + parity * HD
        queries.append(
            widen(jnp.concatenate([turned[:, at : at + HD], turned[:, at + two : at + two + HD]], axis=1))
        )

    def here(i, rows):
        lane = lax.broadcasted_iota(jnp.int32, (rows, window), 1)
        return (lane >= offset + i * HD) & (lane < offset + (i + 1) * HD)

    for parity in range(2):
        product = queries[parity] * own_k
        own = jnp.zeros((extra, window), F32)
        for i in range(2):
            mask = here(i, extra)
            own = own + jnp.where(mask, jnp.sum(jnp.where(mask, product, 0.0), axis=-1, keepdims=True), 0.0)
        rows = slice(parity * requests, (parity + 1) * requests)
        part_ref[2, 0, rows, :] = own_v[:requests]
        part_ref[2, 1, rows, :] = own[:requests] * SCALE
        part_ref[2, 2, rows, :] = jnp.ones((requests, window), F32)

    for r in range(requests):
        query = [
            jnp.where(here(i, 1), queries[parity][r : r + 1], 0.0) for parity in range(2) for i in range(2)
        ]
        query = jnp.concatenate(query + [jnp.zeros((4, window), F32)], axis=0).astype(BF16)
        for b in range(2):
            scores = (
                lax.dot_general(query, k_ref[b, r], (((1,), (1,)), ((), ())), preferred_element_type=F32)
                * SCALE
            )
            live = lax.broadcasted_iota(jnp.int32, scores.shape, 1) + start_ref[b] < len_ref[r]
            scores = jnp.where(live, scores, NEGATIVE)
            peak = jnp.max(scores, axis=-1, keepdims=True)
            expanded = jnp.where(live, jnp.exp(scores - peak), 0.0)
            total = jnp.sum(expanded, axis=-1, keepdims=True)
            sums = jnp.dot(expanded.astype(BF16), v_ref[b, r], preferred_element_type=F32)
            for slot, values in enumerate((sums, peak, total)):
                for parity in range(2):
                    row = parity * requests + r
                    part_ref[b, slot, row : row + 1, :] = sum(
                        jnp.where(here(i, 1), values[2 * parity + i : 2 * parity + i + 1], 0.0) for i in range(2)
                    )


def group_kernel(block_rows, plan, norm, offset, stretches, *refs):
    refs = list(refs)

    def take(count=1):
        taken, refs[:count] = refs[:count], []
        return taken

    with_decode = offset is not None
    (offs_ref,) = take()
    if with_decode:
        lane_ref, len_ref, start_ref = take(3)
    w_refs = take(1 + max(source[0] for sources in plan for source in sources))
    x_hbm = take(stretches)
    (table_ref,) = take()
    if with_decode:
        dx_ref, dtable_ref = take(2)
        caches = take(4)
    o_refs = take(stretches)
    if with_decode:
        (part_ref,) = take()
    if norm:
        xn_hbm = take(stretches)
        (dxn_ref,) = take()
    x_refs, u_refs, heads_refs = take(stretches), take(stretches), take(stretches)
    (w_ref,) = take()
    if with_decode:
        k_ref, v_ref = take(2)
    if norm:
        (gain_ref,) = take()
    (sem,) = take()
    stretch = table_ref.shape[1]
    main = pl.ds(0, stretch)

    if norm:
        fetch(plan[2], w_refs, offs_ref, block_rows, LANES, lambda rows: gain_ref.at[rows], sem.at[1])
    loads = [pltpu.make_async_copy(x_hbm[n], x_refs[n].at[main], sem.at[2 + n]) for n in range(stretches)]
    loads[0].start()
    fetch_weights(plan[:2], w_refs, offs_ref, block_rows, w_ref, sem.at[0])
    for load in loads[1:]:
        load.start()
    if with_decode:
        window = k_ref.shape[3]
        for n, source in enumerate(caches):
            lane = pl.multiple_of(lane_ref[0], LANES) if n < 2 else 0 if offset == 0 else LANES
            pltpu.make_async_copy(
                source.at[:, :, pl.ds(lane, window)], (k_ref, v_ref)[n % 2].at[n // 2], sem.at[4 + n]
            ).start()
    if norm:
        pltpu.make_async_copy(gain_ref, gain_ref, sem.at[1]).wait()
        pick = (lax.broadcasted_iota(jnp.int32, (8, LANES), 1) == 0).astype(BF16)
        gain = lax.dot_general(pick, gain_ref[...], (((1,), (1,)), ((), ())), preferred_element_type=F32)[0:1]
        dxn_ref[...] = normalize(dx_ref[...], gain)
    saves = []
    for n in range(stretches):
        loads[n].wait()
        if norm:
            def body(i, _):
                rows = pl.ds(pl.multiple_of(i * 64, 64), 64)
                x_refs[n][rows, :] = normalize(x_refs[n][rows, :], gain)
                return 0

            lax.fori_loop(0, stretch // 64, body, 0)
            saves.append(pltpu.make_async_copy(x_refs[n].at[main], xn_hbm[n], sem.at[8 + n]))
            saves[-1].start()
        if n == 0:
            pltpu.make_async_copy(w_ref, w_ref, sem.at[0]).wait()
            if with_decode:
                x_refs[0][stretch:, :] = dxn_ref[...] if norm else dx_ref[...]
        multiply(x_refs[n][...], w_ref, u_refs[n], x_refs[n].shape[0])
        store_heads(u_refs[n], table_ref, heads_refs[n], 0)
        if n == 0 and with_decode:
            turned = turn_decode(u_refs[0][stretch:, :], dtable_ref)
            for m, source in enumerate(caches):
                target = (k_ref, v_ref)[m % 2].at[m // 2]
                pltpu.make_async_copy(target, target, sem.at[4 + m]).wait()
            decode(turned, k_ref.shape[1], offset, k_ref, v_ref, len_ref, start_ref, part_ref)
        attend(heads_refs[n], o_refs[n], 256)
    for save in saves:
        save.wait()


def run_group(rows, tables, offs, w_pieces, block_rows, plan, norm=False, decoding=None):
    stretch, depth = rows[0].shape
    stretches = len(rows)
    width = KV * HD
    smem = pl.BlockSpec(memory_space=pltpu.SMEM)
    vmem = pl.BlockSpec(memory_space=pltpu.VMEM)
    hbm = pl.BlockSpec(memory_space=pl.ANY)
    operands, in_specs, offset, extra = [offs], [smem], None, 0
    if decoding:
        offset, lane, cache_len, starts, dx, dtable, caches = decoding
        requests, span = caches[0].shape[:2]
        extra, window = dx.shape[0], 2 * LANES
        operands += [lane, cache_len, starts]
        in_specs += [smem] * 3
    operands += [*w_pieces, *rows, tables]
    in_specs += [hbm] * (len(w_pieces) + stretches) + [vmem]
    out_shape = [jax.ShapeDtypeStruct((stretch, 4 * LANES), BF16)] * stretches
    out_specs = [vmem] * stretches
    if decoding:
        operands += [dx, dtable, *caches]
        in_specs += [vmem] * 2 + [hbm] * 4
        out_shape.append(jax.ShapeDtypeStruct((3, 3, 2 * requests, window), F32))
        out_specs.append(vmem)
    if norm:
        out_shape += [jax.ShapeDtypeStruct((stretch, depth), BF16)] * stretches
        out_shape.append(jax.ShapeDtypeStruct((extra, depth), BF16))
        out_specs += [hbm] * stretches + [vmem]
    rows_all = [stretch + (extra if n == 0 else 0) for n in range(stretches)]
    scratch = [pltpu.VMEM((count, depth), BF16) for count in rows_all]
    scratch += [pltpu.VMEM((count, width), F32) for count in rows_all]
    scratch += [pltpu.VMEM((8, stretch, LANES), BF16)] * stretches
    scratch.append(pltpu.VMEM((depth, width), BF16))
    if decoding:
        scratch += [pltpu.VMEM((2, requests, span, window), BF16)] * 2
    if norm:
        scratch.append(pltpu.VMEM((depth, LANES), BF16))
    scratch.append(pltpu.SemaphoreType.DMA((10,)))
    return pl.pallas_call(
        functools.partial(group_kernel, block_rows, plan, norm, offset, stretches),
        in_specs=in_specs,
        out_specs=out_specs,
        out_shape=out_shape,
        scratch_shapes=scratch,
        compiler_params=pltpu.CompilerParams(vmem_limit_bytes=VMEM_BYTES),
        cost_estimate=cost(10 * stretches),
        name="group",
    )(*operands)


def output_kernel(requests, block_rows, plan, o_plan, core_ref, offs_ref, *rest):
    count = 1 + max(source[0] for sources in plan for source in sources)
    wo_refs = rest[:count]
    o_refs, rest = rest[count : count + len(o_plan)], rest[count + len(o_plan) :]
    parts_ref, other_ref, out_ref, dec_ref, wo_ref, att_ref, w_sem, o_sem = rest
    step = pl.program_id(0)
    stretch = out_ref.shape[0]
    columns = out_ref.shape[1]
    steps = wo_ref.shape[0]
    half = PAD // 2

    @pl.when(step == 0)
    def _():
        me, core = core_ref[0], core_ref[1]
        o_copies = [
            pltpu.make_async_copy(
                source,
                att_ref.at[core if mine else 1 - core, pl.ds(0, stretch), pl.ds(lane, source.shape[1])],
                o_sem.at[n],
            )
            for n, (source, (mine, lane)) in enumerate(zip(o_refs, o_plan))
        ]
        for copy in o_copies:
            copy.start()
        for t, sources in enumerate(plan):
            for ref, column, first, blocks in sources:
                for b in range(blocks):
                    to = pl.multiple_of(offs_ref[first + b], 16)
                    pltpu.make_async_copy(
                        wo_refs[ref].at[pl.ds(b * block_rows, block_rows), pl.ds(column, columns)],
                        wo_ref.at[t, pl.ds(to, block_rows)],
                        w_sem.at[t],
                    ).start()
        for t in range(steps):
            for h in range(H):
                wo_ref[t, h * LANES + HD : (h + 1) * LANES, :] = jnp.zeros((LANES - HD, columns), BF16)
        extra = att_ref.shape[1] - stretch
        att_ref[:, stretch:, :] = jnp.zeros((2, extra, half), BF16)
        chips = parts_ref.shape[0]
        for parts, place in ((parts_ref, core), (other_ref, 1 - core)):
            blocks = [(jnp.bitwise_xor(me // 2, chip), b) for chip in range(chips) for b in range(2)] + [(0, 2)]
            top = parts[0, 2, 1]
            for slot, b in blocks:
                top = jnp.maximum(top, parts[slot, b, 1])
            numerator, denominator = jnp.zeros_like(top), jnp.zeros_like(top)
            for slot, b in blocks:
                rescale = jnp.exp(parts[slot, b, 1] - top)
                numerator = numerator + rescale * parts[slot, b, 0]
                denominator = denominator + rescale * parts[slot, b, 2]
            mix = numerator / jnp.where(denominator > 0.0, denominator, 1.0)
            window = mix.shape[1] // 2
            for parity in range(2):
                rows = mix[parity * requests : (parity + 1) * requests]
                rows = jnp.concatenate([rows, jnp.zeros((extra - requests, mix.shape[1]), F32)], axis=0)
                for g in range(2):
                    for i in range(2):
                        at = g * window + g * (window - 2 * HD) + i * HD
                        to = (4 * g + 2 * i + parity) * LANES
                        att_ref[place, stretch:, to : to + HD] = rows[:, at : at + HD].astype(BF16)
        for copy in o_copies:
            copy.wait()

    for t in range(steps):
        @pl.when(step == t)
        def _():
            whole = wo_ref.at[t, pl.ds(0, H * HD)]
            pltpu.make_async_copy(whole, whole, w_sem.at[t]).wait()

    projected = jnp.dot(att_ref[0], wo_ref[step, :half], preferred_element_type=F32) + jnp.dot(
        att_ref[1], wo_ref[step, half:], preferred_element_type=F32
    )
    out_ref[...] = projected[:stretch].astype(BF16)
    dec_ref[...] = projected[stretch : stretch + requests].astype(BF16)


def output(attended, parts, other_parts, core, offs, wo_pieces, block_rows, plan, requests):
    stretch = attended[0][0].shape[0]
    width = H * HD
    steps, extra = 2, 16
    smem = pl.BlockSpec(memory_space=pltpu.SMEM)
    vmem = pl.BlockSpec(memory_space=pltpu.VMEM)
    hbm = pl.BlockSpec(memory_space=pl.ANY)
    return pl.pallas_call(
        functools.partial(output_kernel, requests, block_rows, plan, [piece[1:] for piece in attended]),
        grid=(steps,),
        in_specs=[smem] * 2 + [hbm] * (len(wo_pieces) + len(attended)) + [vmem] * 2,
        out_specs=[
            pl.BlockSpec((stretch, width // steps), lambda t: (0, t)),
            pl.BlockSpec((requests, width // steps), lambda t: (0, t)),
        ],
        out_shape=[
            jax.ShapeDtypeStruct((stretch, width), BF16),
            jax.ShapeDtypeStruct((requests, width), BF16),
        ],
        scratch_shapes=[
            pltpu.VMEM((steps, PAD, width // steps), BF16),
            pltpu.VMEM((2, stretch + extra, PAD // 2), BF16),
            pltpu.SemaphoreType.DMA((steps,)),
            pltpu.SemaphoreType.DMA((len(attended),)),
        ],
        compiler_params=pltpu.CompilerParams(
            dimension_semantics=("arbitrary",), vmem_limit_bytes=VMEM_BYTES
        ),
        cost_estimate=cost(9),
        name="output",
    )(core, offs, *wo_pieces, *[piece[0] for piece in attended], parts, other_parts)


def swap(array, mask, n_shard):
    return lax.ppermute(array, "shard", [(i, i ^ mask) for i in range(n_shard)])


def after(array, *others):
    return lax.optimization_barrier((array, *others))[0]


def along_dp(local, n_dp):
    found = [local]
    for shift in range(1, n_dp):
        found.append(lax.ppermute(local, "dp", [((i + shift) % n_dp, i) for i in range(n_dp)]))
    return jnp.concatenate(found, axis=0)


def pieces_of(here, beside, above, cut, n_shard):
    whole = here.shape[1]
    left, right = swap(beside[:, :cut], 4, n_shard), swap(above[:, cut:], 2, n_shard)
    return [(here, 0, 0, whole), (beside, 1, 0, whole), (above, 2, 0, whole), (left, 3, 0, cut), (right, 3, cut, whole)]


def lay_out(pieces, starts, n_dp, first=0):
    plan = [[] for _ in starts]
    for index, (_, mask, left, right) in enumerate(pieces):
        for column, t in starts.items():
            if left <= column < right:
                plan[t].append((index, column - left, mask * n_dp, n_dp))
    return plan


def group_columns(wqkv, core, width):
    quarter = width // 4
    found = []
    for g in range(2):
        at = (2 * core + g) * quarter
        found += [
            wqkv[:, 2 * width + at : 2 * width + at + quarter],
            wqkv[:, 3 * width + at : 3 * width + at + quarter],
            wqkv[:, 2 * at : 2 * at + 2 * quarter],
        ]
    return jnp.concatenate(found, axis=1)


def per_device(n_dp, n_shard, prefill_x, decode_x, norm_gain, wqkv, wo, k_cache, v_cache, cache_len):
    stretch = prefill_x.shape[0]
    requests, span, width = k_cache.shape
    half = width // 2
    me, me_dp = lax.axis_index("shard"), lax.axis_index("dp")
    core = me % 2
    everyone = ("dp", "shard")
    block_rows = wqkv.shape[0]
    low, high = group_columns(wqkv, 0, width), group_columns(wqkv, 1, width)
    gain_columns = jnp.broadcast_to(norm_gain[:, None], (block_rows, LANES))
    head = LANES + width
    split = n_shard == 8 and block_rows == HALF

    wo_all = lax.all_gather(wo, everyone, axis=0, tiled=True)
    wo_plan = [[(0, 0, 0, H)], [(0, width, 0, H)]]
    wo_offs = jnp.arange(H, dtype=jnp.int32) * LANES
    sib_x = swap(prefill_x, 1, n_shard)
    sib_caches = [
        swap(jnp.where(core == 0, cache[:, :, half:], cache[:, :, :half]), 1, n_shard) for cache in (k_cache, v_cache)
    ]
    extra = 16
    dx = jnp.pad(decode_x, ((0, extra - requests), (0, 0)))
    decode_positions = jnp.concatenate([cache_len, jnp.zeros((extra - requests,), jnp.int32)])
    tables = rope_tables(jnp.arange(stretch, dtype=jnp.int32), LANES)
    turning = rope_tables(decode_positions, half)
    quarter = half // 2
    plain = jnp.stack([jnp.ones((extra, quarter), F32)] + [jnp.zeros((extra, quarter), F32)] * 2)
    dtable = jnp.concatenate([turning[:, :, :quarter], plain, turning], axis=2)
    if split:
        first = core == 0
        mine = jnp.concatenate([gain_columns, jnp.where(first, low, high)], axis=1)
        theirs = jnp.concatenate([gain_columns, jnp.where(first, high, low)], axis=1)
        theirs = swap(theirs, 1, n_shard)
        pair = jnp.concatenate([jnp.where(first, mine, theirs), jnp.where(first, theirs, mine)], axis=0)
        order = jnp.arange(n_shard // 2 * n_dp, dtype=jnp.int32)
        chip = (me_dp + order % n_dp) % n_dp * (n_shard // 2) + (me // 2 ^ (order // n_dp))
        block_rows = 2 * block_rows
        offs = chip * block_rows
        here = along_dp(pair[:, :head], n_dp)
        beside, above = swap(here, 2, n_shard), swap(here, 4, n_shard)
        later_here = along_dp(after(pair[:, head:], beside, above), n_dp)
        pieces = pieces_of(here, beside, above, LANES + half, n_shard)
        plan = lay_out(pieces, {LANES: 0, LANES + half: 1, 0: 2}, n_dp)
        pieces = [piece[0] for piece in pieces]
        later_here = after(later_here, *pieces)
        beside, above = swap(later_here, 2, n_shard), swap(later_here, 4, n_shard)
    else:
        offs = jnp.zeros((1,), jnp.int32)
        every = lax.all_gather(jnp.concatenate([gain_columns, low, high], axis=1), everyone, axis=0, tiled=True)
        block_rows = every.shape[0]
        chosen = jnp.where(core == 0, every[:, LANES : LANES + 2 * width], every[:, LANES + 2 * width :])
        pieces = [jnp.concatenate([every[:, :LANES], chosen[:, :width]], axis=1)]
        plan = [[(0, LANES, 0, 1)], [(0, LANES + half, 0, 1)], [(0, 0, 0, 1)]]

    lane = core.astype(jnp.int32).reshape(1) * half
    starts = jnp.stack([me * span, (me ^ 1) * span]).astype(jnp.int32)
    caches = [k_cache, v_cache, *sib_caches]
    own_o, sib_o, part, xn, sib_xn, dxn = run_group(
        [prefill_x, sib_x], tables, offs, pieces, block_rows, plan, norm=True,
        decoding=(0, lane, cache_len, starts, dx, dtable, caches),
    )
    mine, theirs = [own_o], [sib_o]
    if split:
        pieces = pieces_of(later_here, after(beside, sib_o), after(above, sib_o), half, n_shard)
        plan = lay_out(pieces, {0: 0, half: 1}, n_dp)
        pieces = [piece[0] for piece in pieces]
    else:
        pieces = [chosen[:, width:]]
        plan = [[(0, 0, 0, 1)], [(0, half, 0, 1)]]
    sib_o, later_part = run_group(
        [sib_xn], tables, offs, pieces, block_rows, plan,
        decoding=(LANES // 2, lane + LANES, cache_len, starts, dxn, dtable, caches),
    )
    theirs.append(sib_o)
    part = jnp.concatenate([part, later_part], axis=-1)
    parts = jnp.stack([part] + [swap(part, 2 * chip, n_shard) for chip in range(1, n_shard // 2)])
    mine += run_group([after(xn, sib_o)], tables, offs, pieces, block_rows, plan)
    other_parts = swap(after(parts, mine[1]), 1, n_shard)
    group_lanes = PAD // 4
    attended = [(piece, True, g * group_lanes) for g, piece in enumerate(mine)]
    attended += [(swap(piece, 1, n_shard), False, g * group_lanes) for g, piece in enumerate(theirs)]
    me_and_core = jnp.stack([me, core]).astype(jnp.int32)
    return output(attended, parts, other_parts, me_and_core, wo_offs, [wo_all], HD, wo_plan, requests)


def solution(mesh):
    in_specs = (
        P(("dp", "shard"), None),
        P("dp", None),
        P(("dp", "shard")),
        P(("dp", "shard"), None),
        P(("dp", "shard"), None),
        P("dp", "shard", None),
        P("dp", "shard", None),
        P("dp"),
    )
    out_specs = (P(("dp", "shard"), None), P("dp", None))
    return jax.shard_map(
        functools.partial(per_device, mesh.shape["dp"], mesh.shape["shard"]),
        mesh=mesh, in_specs=in_specs, out_specs=out_specs, check_vma=False,
    )
```

```python
import functools

import jax
import jax.numpy as jnp
from jax import lax
from jax.experimental import pallas as pl
from jax.experimental.pallas import tpu as pltpu
from jax.sharding import PartitionSpec as P

H = 16
KV = 8
HD = 96
HALF = HD // 2
LANES = 128
PAD = H * LANES

THETA = 100000.0
EPS = 1e-05
NEGATIVE = -1e30
SCALE = HD ** (-0.5)
LOG2E = 1.4426950408889634

BF16 = jnp.bfloat16
F32 = jnp.float32
VMEM_BYTES = 56 * 1024 * 1024


def cost(microseconds):
    return pl.CostEstimate(flops=int(microseconds * 1.1e9), bytes_accessed=100_000, transcendentals=0)


def rope_tables(positions, width):
    lane = jnp.arange(width, dtype=jnp.int32)
    lane = lane % HD if width % HD == 0 else lane
    frequency = jnp.power(THETA, -(lane % HALF).astype(F32) * (2.0 / HD))
    angles = positions.astype(F32)[:, None] * frequency[None, :]
    cosine, sine = jnp.cos(angles), jnp.sin(angles)
    lane = lane[None, :]
    return jnp.stack(
        [
            jnp.where(lane < HD, cosine, 0.0),
            jnp.where((lane >= HALF) & (lane < HD), sine, 0.0),
            jnp.where(lane < HALF, -sine, 0.0),
        ]
    )


def normalize(rows, gain):
    widened = rows.astype(F32)
    factor = lax.rsqrt(jnp.mean(widened * widened, axis=-1, keepdims=True) + EPS)
    return (widened * factor * gain).astype(BF16)


def head_tile(u_ref, rows, index):
    base, place = (index // 4) * 3 * LANES, index % 4
    lane = lax.broadcasted_iota(jnp.int32, (rows.stop - rows.start, LANES), 1)

    def tile(t):
        return u_ref[rows, base + t * LANES : base + (t + 1) * LANES]

    if place == 0:
        return tile(0)
    if place == 1:
        return pltpu.roll(jnp.where(lane >= 96, tile(0), tile(1)), 32, 1)
    if place == 2:
        return pltpu.roll(jnp.where(lane >= 64, tile(1), tile(2)), 64, 1)
    return pltpu.roll(tile(2), 96, 1)


def fetch(sources, refs, offs_ref, block_rows, columns, target, sem):
    for ref, column, first, blocks in sources:
        for b in range(blocks):
            to = pl.ds(pl.multiple_of(offs_ref[first + b], 16), block_rows)
            source = refs[ref].at[pl.ds(b * block_rows, block_rows), pl.ds(column, columns)]
            pltpu.make_async_copy(source, target(to), sem).start()


def fetch_weights(plan, refs, offs_ref, block_rows, w_ref, sem):
    half = w_ref.shape[1] // len(plan)
    for t, sources in enumerate(plan):
        fetch(sources, refs, offs_ref, block_rows, half, lambda rows: w_ref.at[rows, pl.ds(t * half, half)], sem)


def multiply(x, w_ref, u_ref, rows):
    for n in range(w_ref.shape[1] // 256):
        cols = slice(n * 256, (n + 1) * 256)
        u_ref[:rows, cols] = jnp.dot(x, w_ref[:, cols], preferred_element_type=F32)


def store_heads(u_ref, table_ref, heads_ref, first):
    rows = table_ref.shape[1]
    lane = lax.broadcasted_iota(jnp.int32, (rows, LANES), 1)
    for h in range(8):
        u = head_tile(u_ref, slice(0, rows), h)
        if h in (2, 3):
            u = jnp.where(lane < HD, u, 1.0)
        else:
            u = (
                u * table_ref[0]
                + pltpu.roll(u, HALF, 1) * table_ref[1]
                + pltpu.roll(u, LANES - HALF, 1) * table_ref[2]
            )
        heads_ref[h, first : first + rows, :] = u.astype(BF16)


def turn_decode(u, dtable_ref):
    return (
        u * dtable_ref[0]
        + pltpu.roll(u, HALF, 1) * dtable_ref[1]
        + pltpu.roll(u, u.shape[1] - HALF, 1) * dtable_ref[2]
    ).astype(BF16)


def attend(heads_ref, o_ref, block):
    stretch = o_ref.shape[0]
    causal = lax.broadcasted_iota(jnp.int32, (block, block), 1) <= lax.broadcasted_iota(
        jnp.int32, (block, block), 0
    )
    causal = jnp.concatenate([causal, causal], axis=0)
    for j in range(2):
        for i in range(stretch // block):
            rows = slice(i * block, (i + 1) * block)
            seen = (i + 1) * block
            both = heads_ref[4 + 2 * j : 6 + 2 * j, rows, :].reshape(2 * block, LANES)
            scores = lax.dot_general(
                both, heads_ref[j, :seen, :], (((1,), (1,)), ((), ())), preferred_element_type=F32
            )
            last = jnp.where(causal, scores[:, i * block :], NEGATIVE)
            scores = last if i == 0 else jnp.concatenate([scores[:, : i * block], last], axis=1)
            peak = jnp.max(scores, axis=-1, keepdims=True)
            weights = jnp.exp2((scores - peak) * (SCALE * LOG2E)).astype(BF16)
            mixed = jnp.dot(weights, heads_ref[2 + j, :seen, :], preferred_element_type=F32)
            mixed = (mixed / mixed[:, HD : HD + 1]).astype(BF16)
            for parity in range(2):
                lanes = slice((2 * j + parity) * LANES, (2 * j + parity + 1) * LANES)
                o_ref[rows, lanes] = mixed[parity * block : (parity + 1) * block]


def decode(turned, requests, offset, k_ref, v_ref, len_ref, start_ref, part_ref):
    turned = turned.astype(F32)
    extra = turned.shape[0]
    window, span = k_ref.shape[3], k_ref.shape[2]
    two = 2 * HD

    def widen(values):
        sides = [jnp.zeros((extra, offset), F32)] if offset else []
        sides += [values]
        sides += [jnp.zeros((extra, window - two - offset), F32)] if window - two - offset else []
        return jnp.concatenate(sides, axis=1)

    own_k, own_v = widen(turned[:, :two]), widen(turned[:, two : 2 * two])
    queries = []
    for parity in range(2):
        at = 2 * two + parity * HD
        queries.append(
            widen(jnp.concatenate([turned[:, at : at + HD], turned[:, at + two : at + two + HD]], axis=1))
        )

    def here(i, rows):
        lane = lax.broadcasted_iota(jnp.int32, (rows, window), 1)
        return (lane >= offset + i * HD) & (lane < offset + (i + 1) * HD)

    for parity in range(2):
        product = queries[parity] * own_k
        own = jnp.zeros((extra, window), F32)
        for i in range(2):
            mask = here(i, extra)
            own = own + jnp.where(mask, jnp.sum(jnp.where(mask, product, 0.0), axis=-1, keepdims=True), 0.0)
        rows = slice(parity * requests, (parity + 1) * requests)
        part_ref[2, 0, rows, :] = own_v[:requests]
        part_ref[2, 1, rows, :] = own[:requests] * SCALE
        part_ref[2, 2, rows, :] = jnp.ones((requests, window), F32)

    for r in range(requests):
        query = [
            jnp.where(here(i, 1), queries[parity][r : r + 1], 0.0) for parity in range(2) for i in range(2)
        ]
        query = jnp.concatenate(query + [jnp.zeros((4, window), F32)], axis=0).astype(BF16)
        for b in range(2):
            scores = (
                lax.dot_general(query, k_ref[b, r], (((1,), (1,)), ((), ())), preferred_element_type=F32)
                * SCALE
            )
            live = lax.broadcasted_iota(jnp.int32, scores.shape, 1) + start_ref[b] < len_ref[r]
            scores = jnp.where(live, scores, NEGATIVE)
            peak = jnp.max(scores, axis=-1, keepdims=True)
            expanded = jnp.where(live, jnp.exp(scores - peak), 0.0)
            total = jnp.sum(expanded, axis=-1, keepdims=True)
            sums = jnp.dot(expanded.astype(BF16), v_ref[b, r], preferred_element_type=F32)
            for slot, values in enumerate((sums, peak, total)):
                for parity in range(2):
                    row = parity * requests + r
                    part_ref[b, slot, row : row + 1, :] = sum(
                        jnp.where(here(i, 1), values[2 * parity + i : 2 * parity + i + 1], 0.0) for i in range(2)
                    )


def group_kernel(block_rows, plan, norm, offset, stretches, *refs):
    refs = list(refs)

    def take(count=1):
        taken, refs[:count] = refs[:count], []
        return taken

    with_decode = offset is not None
    (offs_ref,) = take()
    if with_decode:
        lane_ref, len_ref, start_ref = take(3)
    w_refs = take(1 + max(source[0] for sources in plan for source in sources))
    x_hbm = take(stretches)
    (table_ref,) = take()
    if with_decode:
        dx_ref, dtable_ref = take(2)
        caches = take(4)
    o_refs = take(stretches)
    if with_decode:
        (part_ref,) = take()
    if norm:
        xn_hbm = take(stretches)
        if with_decode:
            (dxn_ref,) = take()
    x_refs, u_refs, heads_refs = take(stretches), take(stretches), take(stretches)
    (w_ref,) = take()
    if with_decode:
        k_ref, v_ref = take(2)
    if norm:
        (gain_ref,) = take()
    (sem,) = take()
    stretch = table_ref.shape[1]
    main = pl.ds(0, stretch)

    if norm:
        fetch(plan[2], w_refs, offs_ref, block_rows, LANES, lambda rows: gain_ref.at[rows], sem.at[1])
    loads = [pltpu.make_async_copy(x_hbm[n], x_refs[n].at[main], sem.at[2 + n]) for n in range(stretches)]
    loads[0].start()
    fetch_weights(plan[:2], w_refs, offs_ref, block_rows, w_ref, sem.at[0])
    for load in loads[1:]:
        load.start()
    if with_decode:
        window = k_ref.shape[3]
        for n, source in enumerate(caches):
            lane = pl.multiple_of(lane_ref[0], LANES)
            pltpu.make_async_copy(
                source.at[:, :, pl.ds(lane, window)], (k_ref, v_ref)[n % 2].at[n // 2], sem.at[4 + n]
            ).start()
    if norm:
        pltpu.make_async_copy(gain_ref, gain_ref, sem.at[1]).wait()
        pick = (lax.broadcasted_iota(jnp.int32, (8, LANES), 1) == 0).astype(BF16)
        gain = lax.dot_general(pick, gain_ref[...], (((1,), (1,)), ((), ())), preferred_element_type=F32)[0:1]
        if with_decode:
            dxn_ref[...] = normalize(dx_ref[...], gain)
    saves = []
    for n in range(stretches):
        loads[n].wait()
        if norm:
            def body(i, _):
                rows = pl.ds(pl.multiple_of(i * 64, 64), 64)
                x_refs[n][rows, :] = normalize(x_refs[n][rows, :], gain)
                return 0

            lax.fori_loop(0, stretch // 64, body, 0)
            saves.append(pltpu.make_async_copy(x_refs[n].at[main], xn_hbm[n], sem.at[8 + n]))
            saves[-1].start()
        if n == 0:
            pltpu.make_async_copy(w_ref, w_ref, sem.at[0]).wait()
            if with_decode:
                x_refs[0][stretch:, :] = dxn_ref[...] if norm else dx_ref[...]
        multiply(x_refs[n][...], w_ref, u_refs[n], x_refs[n].shape[0])
        store_heads(u_refs[n], table_ref, heads_refs[n], 0)
        if n == 0 and with_decode:
            turned = turn_decode(u_refs[0][stretch:, :], dtable_ref)
            for m, source in enumerate(caches):
                target = (k_ref, v_ref)[m % 2].at[m // 2]
                pltpu.make_async_copy(target, target, sem.at[4 + m]).wait()
            decode(turned, k_ref.shape[1], offset, k_ref, v_ref, len_ref, start_ref, part_ref)
        attend(heads_refs[n], o_refs[n], 256)
    for save in saves:
        save.wait()


def run_group(rows, tables, offs, w_pieces, block_rows, plan, norm=False, decoding=None):
    stretch, depth = rows[0].shape
    stretches = len(rows)
    width = KV * HD
    smem = pl.BlockSpec(memory_space=pltpu.SMEM)
    vmem = pl.BlockSpec(memory_space=pltpu.VMEM)
    hbm = pl.BlockSpec(memory_space=pl.ANY)
    operands, in_specs, offset, extra = [offs], [smem], None, 0
    if decoding:
        offset, lane, cache_len, starts, dx, dtable, caches = decoding
        requests, span = caches[0].shape[:2]
        extra, window = dx.shape[0], 2 * LANES
        operands += [lane, cache_len, starts]
        in_specs += [smem] * 3
    operands += [*w_pieces, *rows, tables]
    in_specs += [hbm] * (len(w_pieces) + stretches) + [vmem]
    out_shape = [jax.ShapeDtypeStruct((stretch, 4 * LANES), BF16)] * stretches
    out_specs = [vmem] * stretches
    if decoding:
        operands += [dx, dtable, *caches]
        in_specs += [vmem] * 2 + [hbm] * 4
        out_shape.append(jax.ShapeDtypeStruct((3, 3, 2 * requests, window), F32))
        out_specs.append(vmem)
    if norm:
        out_shape += [jax.ShapeDtypeStruct((stretch, depth), BF16)] * stretches
        out_specs += [hbm] * stretches
        if decoding:
            out_shape.append(jax.ShapeDtypeStruct((extra, depth), BF16))
            out_specs.append(vmem)
    rows_all = [stretch + (extra if n == 0 else 0) for n in range(stretches)]
    scratch = [pltpu.VMEM((count, depth), BF16) for count in rows_all]
    scratch += [pltpu.VMEM((count, width), F32) for count in rows_all]
    scratch += [pltpu.VMEM((8, stretch, LANES), BF16)] * stretches
    scratch.append(pltpu.VMEM((depth, width), BF16))
    if decoding:
        scratch += [pltpu.VMEM((2, requests, span, window), BF16)] * 2
    if norm:
        scratch.append(pltpu.VMEM((depth, LANES), BF16))
    scratch.append(pltpu.SemaphoreType.DMA((10,)))
    return pl.pallas_call(
        functools.partial(group_kernel, block_rows, plan, norm, offset, stretches),
        in_specs=in_specs,
        out_specs=out_specs,
        out_shape=out_shape,
        scratch_shapes=scratch,
        compiler_params=pltpu.CompilerParams(vmem_limit_bytes=VMEM_BYTES),
        cost_estimate=cost(10 * stretches),
        name="group",
    )(*operands)


def output_kernel(requests, block_rows, plan, o_plan, core_ref, offs_ref, *rest):
    count = 1 + max(source[0] for sources in plan for source in sources)
    wo_refs = rest[:count]
    o_refs, rest = rest[count : count + len(o_plan)], rest[count + len(o_plan) :]
    parts_ref, other_ref, out_ref, dec_ref, wo_ref, att_ref, w_sem, o_sem = rest
    step = pl.program_id(0)
    stretch = out_ref.shape[0]
    columns = out_ref.shape[1]
    steps = wo_ref.shape[0]
    half = PAD // 2

    @pl.when(step == 0)
    def _():
        me, core = core_ref[0], core_ref[1]
        o_copies = [
            pltpu.make_async_copy(
                source,
                att_ref.at[core if mine else 1 - core, pl.ds(0, stretch), pl.ds(lane, source.shape[1])],
                o_sem.at[n],
            )
            for n, (source, (mine, lane)) in enumerate(zip(o_refs, o_plan))
        ]
        for copy in o_copies:
            copy.start()
        for t, sources in enumerate(plan):
            for ref, column, first, blocks in sources:
                for b in range(blocks):
                    to = pl.multiple_of(offs_ref[first + b], 16)
                    pltpu.make_async_copy(
                        wo_refs[ref].at[pl.ds(b * block_rows, block_rows), pl.ds(column, columns)],
                        wo_ref.at[t, pl.ds(to, block_rows)],
                        w_sem.at[t],
                    ).start()
        for t in range(steps):
            for h in range(H):
                wo_ref[t, h * LANES + HD : (h + 1) * LANES, :] = jnp.zeros((LANES - HD, columns), BF16)
        extra = att_ref.shape[1] - stretch
        att_ref[:, stretch:, :] = jnp.zeros((2, extra, half), BF16)
        chips = parts_ref.shape[0]
        for parts, place in ((parts_ref, core), (other_ref, 1 - core)):
            blocks = [(jnp.bitwise_xor(me // 2, chip), b) for chip in range(chips) for b in range(2)] + [(0, 2)]
            top = parts[0, 2, 1]
            for slot, b in blocks:
                top = jnp.maximum(top, parts[slot, b, 1])
            numerator, denominator = jnp.zeros_like(top), jnp.zeros_like(top)
            for slot, b in blocks:
                rescale = jnp.exp(parts[slot, b, 1] - top)
                numerator = numerator + rescale * parts[slot, b, 0]
                denominator = denominator + rescale * parts[slot, b, 2]
            mix = numerator / jnp.where(denominator > 0.0, denominator, 1.0)
            window = mix.shape[1] // 2
            for parity in range(2):
                rows = mix[parity * requests : (parity + 1) * requests]
                rows = jnp.concatenate([rows, jnp.zeros((extra - requests, mix.shape[1]), F32)], axis=0)
                for g in range(2):
                    for i in range(2):
                        at = g * window + g * (window - 2 * HD) + i * HD
                        to = (4 * g + 2 * i + parity) * LANES
                        att_ref[place, stretch:, to : to + HD] = rows[:, at : at + HD].astype(BF16)
        for copy in o_copies:
            copy.wait()

    for t in range(steps):
        @pl.when(step == t)
        def _():
            whole = wo_ref.at[t, pl.ds(0, H * HD)]
            pltpu.make_async_copy(whole, whole, w_sem.at[t]).wait()

    projected = jnp.dot(att_ref[0], wo_ref[step, :half], preferred_element_type=F32) + jnp.dot(
        att_ref[1], wo_ref[step, half:], preferred_element_type=F32
    )
    out_ref[...] = projected[:stretch].astype(BF16)
    dec_ref[...] = projected[stretch : stretch + requests].astype(BF16)


def output(attended, parts, other_parts, core, offs, wo_pieces, block_rows, plan, requests):
    stretch = attended[0][0].shape[0]
    width = H * HD
    steps, extra = 2, 16
    smem = pl.BlockSpec(memory_space=pltpu.SMEM)
    vmem = pl.BlockSpec(memory_space=pltpu.VMEM)
    hbm = pl.BlockSpec(memory_space=pl.ANY)
    return pl.pallas_call(
        functools.partial(output_kernel, requests, block_rows, plan, [piece[1:] for piece in attended]),
        grid=(steps,),
        in_specs=[smem] * 2 + [hbm] * (len(wo_pieces) + len(attended)) + [vmem] * 2,
        out_specs=[
            pl.BlockSpec((stretch, width // steps), lambda t: (0, t)),
            pl.BlockSpec((requests, width // steps), lambda t: (0, t)),
        ],
        out_shape=[
            jax.ShapeDtypeStruct((stretch, width), BF16),
            jax.ShapeDtypeStruct((requests, width), BF16),
        ],
        scratch_shapes=[
            pltpu.VMEM((steps, PAD, width // steps), BF16),
            pltpu.VMEM((2, stretch + extra, PAD // 2), BF16),
            pltpu.SemaphoreType.DMA((steps,)),
            pltpu.SemaphoreType.DMA((len(attended),)),
        ],
        compiler_params=pltpu.CompilerParams(
            dimension_semantics=("arbitrary",), vmem_limit_bytes=VMEM_BYTES
        ),
        cost_estimate=cost(9),
        name="output",
    )(core, offs, *wo_pieces, *[piece[0] for piece in attended], parts, other_parts)


def swap(array, mask, n_shard):
    return lax.ppermute(array, "shard", [(i, i ^ mask) for i in range(n_shard)])


def after(array, *others):
    return lax.optimization_barrier((array, *others))[0]


def along_dp(local, n_dp):
    found = [local]
    for shift in range(1, n_dp):
        found.append(lax.ppermute(local, "dp", [((i + shift) % n_dp, i) for i in range(n_dp)]))
    return found


def pieces_of(here, beside, above, cut, n_shard):
    whole = here.shape[1]
    left, right = swap(beside[:, :cut], 4, n_shard), swap(above[:, cut:], 2, n_shard)
    return [(here, 0, 0, whole), (beside, 1, 0, whole), (above, 2, 0, whole), (left, 3, 0, cut), (right, 3, cut, whole)]


def lay_out(pieces, starts, n_dp, first=0):
    plan = [[] for _ in starts]
    for index, (_, mask, left, right) in enumerate(pieces):
        for column, t in starts.items():
            if left <= column < right:
                plan[t].append((index, column - left, mask * n_dp, n_dp))
    return plan


def group_columns(wqkv, core, width):
    quarter = width // 4
    found = []
    for g in range(2):
        at = (2 * core + g) * quarter
        found += [
            wqkv[:, 2 * width + at : 2 * width + at + quarter],
            wqkv[:, 3 * width + at : 3 * width + at + quarter],
            wqkv[:, 2 * at : 2 * at + 2 * quarter],
        ]
    return jnp.concatenate(found, axis=1)


def per_device(n_dp, n_shard, prefill_x, decode_x, norm_gain, wqkv, wo, k_cache, v_cache, cache_len):
    stretch = prefill_x.shape[0]
    requests, span, width = k_cache.shape
    half = width // 2
    me, me_dp = lax.axis_index("shard"), lax.axis_index("dp")
    core = me % 2
    everyone = ("dp", "shard")
    block_rows = wqkv.shape[0]
    low, high = group_columns(wqkv, 0, width), group_columns(wqkv, 1, width)
    gain_columns = jnp.broadcast_to(norm_gain[:, None], (block_rows, LANES))
    head = LANES + width
    split = n_shard == 8 and block_rows == HALF

    wo_all = lax.all_gather(wo, everyone, axis=0, tiled=True)
    wo_plan = [[(0, 0, 0, H)], [(0, width, 0, H)]]
    wo_offs = jnp.arange(H, dtype=jnp.int32) * LANES
    extra = 16
    dx = jnp.pad(decode_x, ((0, extra - requests), (0, 0)))
    decode_positions = jnp.concatenate([cache_len, jnp.zeros((extra - requests,), jnp.int32)])
    tables = rope_tables(jnp.arange(stretch, dtype=jnp.int32), LANES)
    turning = rope_tables(decode_positions, half)
    quarter = half // 2
    plain = jnp.stack([jnp.ones((extra, quarter), F32)] + [jnp.zeros((extra, quarter), F32)] * 2)
    dtable = jnp.concatenate([turning[:, :, :quarter], plain, turning], axis=2)
    if split:
        first = core == 0
        mine = jnp.concatenate([gain_columns, jnp.where(first, low, high)], axis=1)
        theirs = jnp.concatenate([gain_columns, jnp.where(first, high, low)], axis=1)
        theirs = swap(theirs, 1, n_shard)
        free = theirs
        pair = jnp.concatenate([jnp.where(first, mine, theirs), jnp.where(first, theirs, mine)], axis=0)
        order = jnp.arange(n_shard // 2 * n_dp, dtype=jnp.int32)
        chip = (me_dp + order % n_dp) % n_dp * (n_shard // 2) + (me // 2 ^ (order // n_dp))
        block_rows = 2 * block_rows
        offs = chip * block_rows
        found = along_dp(pair, n_dp)
        here = jnp.concatenate([block[:, :head] for block in found], axis=0)
        beside, above = swap(here, 2, n_shard), swap(here, 4, n_shard)
        pieces = pieces_of(here, beside, above, LANES + half, n_shard)
        plan = lay_out(pieces, {LANES: 0, LANES + half: 1, 0: 2}, n_dp)
        pieces = [piece[0] for piece in pieces]
        found[0] = after(found[0], beside)
        later_here = jnp.concatenate([block[:, head:] for block in found], axis=0)
        later_here = after(later_here, *pieces)
        beside, above = swap(later_here, 2, n_shard), swap(later_here, 4, n_shard)
    else:
        free = norm_gain
        offs = jnp.zeros((1,), jnp.int32)
        every = lax.all_gather(jnp.concatenate([gain_columns, low, high], axis=1), everyone, axis=0, tiled=True)
        block_rows = every.shape[0]
        chosen = jnp.where(core == 0, every[:, LANES : LANES + 2 * width], every[:, LANES + 2 * width :])
        pieces = [jnp.concatenate([every[:, :LANES], chosen[:, :width]], axis=1)]
        plan = [[(0, LANES, 0, 1)], [(0, LANES + half, 0, 1)], [(0, 0, 0, 1)]]

    sib_x, sib_k, sib_v = [swap(after(array, free), 1, n_shard) for array in (prefill_x, k_cache, v_cache)]
    lane = core.astype(jnp.int32).reshape(1) * half
    starts = jnp.stack([me * span, (me ^ 1) * span]).astype(jnp.int32)
    caches = [k_cache, v_cache, sib_k, sib_v]
    sib_o, part, sib_xn, dxn = run_group(
        [sib_x], tables, offs, pieces, block_rows, plan, norm=True,
        decoding=(0, lane, cache_len, starts, dx, dtable, caches),
    )
    later_pieces, later_plan = [], [[(0, 0, 0, 1)], [(0, half, 0, 1)]]
    if split:
        later_pieces = pieces_of(later_here, after(beside, sib_o), after(above, sib_o), half, n_shard)
        later_plan = lay_out(later_pieces, {0: 0, half: 1}, n_dp)
        later_pieces = [piece[0] for piece in later_pieces]
    else:
        later_pieces = [chosen[:, width:]]
    own_o, xn = run_group([after(prefill_x, sib_o)], tables, offs, pieces, block_rows, plan, norm=True)
    mine, theirs = [own_o], [sib_o]
    pieces, plan = [after(later_pieces[0], own_o)] + later_pieces[1:], later_plan
    sib_o, later_part = run_group(
        [sib_xn], tables, offs, pieces, block_rows, plan,
        decoding=(LANES // 2, lane + LANES, cache_len, starts, dxn, dtable, caches),
    )
    theirs.append(sib_o)
    part = jnp.concatenate([part, later_part], axis=-1)
    parts = jnp.stack([part] + [swap(part, 2 * chip, n_shard) for chip in range(1, n_shard // 2)])
    mine += run_group([after(xn, sib_o)], tables, offs, pieces, block_rows, plan)
    other_parts = swap(after(parts, mine[1]), 1, n_shard)
    group_lanes = PAD // 4
    attended = [(piece, True, g * group_lanes) for g, piece in enumerate(mine)]
    attended += [(swap(piece, 1, n_shard), False, g * group_lanes) for g, piece in enumerate(theirs)]
    me_and_core = jnp.stack([me, core]).astype(jnp.int32)
    return output(attended, parts, other_parts, me_and_core, wo_offs, [wo_all], HD, wo_plan, requests)


def solution(mesh):
    in_specs = (
        P(("dp", "shard"), None),
        P("dp", None),
        P(("dp", "shard")),
        P(("dp", "shard"), None),
        P(("dp", "shard"), None),
        P("dp", "shard", None),
        P("dp", "shard", None),
        P("dp"),
    )
    out_specs = (P(("dp", "shard"), None), P("dp", None))
    return jax.shard_map(
        functools.partial(per_device, mesh.shape["dp"], mesh.shape["shard"]),
        mesh=mesh, in_specs=in_specs, out_specs=out_specs, check_vma=False,
    )
```

```python
import functools

import jax
import jax.numpy as jnp
from jax import lax
from jax.experimental import pallas as pl
from jax.experimental.pallas import tpu as pltpu
from jax.sharding import PartitionSpec as P

H = 16
KV = 8
HD = 96
HALF = HD // 2
LANES = 128
PAD = H * LANES

THETA = 100000.0
EPS = 1e-05
NEGATIVE = -1e30
SCALE = HD ** (-0.5)
LOG2E = 1.4426950408889634

BF16 = jnp.bfloat16
F32 = jnp.float32
VMEM_BYTES = 56 * 1024 * 1024


def cost(microseconds):
    return pl.CostEstimate(flops=int(microseconds * 1.1e9), bytes_accessed=100_000, transcendentals=0)


def rope_tables(positions, width):
    lane = jnp.arange(width, dtype=jnp.int32)
    lane = lane % HD if width % HD == 0 else lane
    frequency = jnp.power(THETA, -(lane % HALF).astype(F32) * (2.0 / HD))
    angles = positions.astype(F32)[:, None] * frequency[None, :]
    cosine, sine = jnp.cos(angles), jnp.sin(angles)
    lane = lane[None, :]
    return jnp.stack(
        [
            jnp.where(lane < HD, cosine, 0.0),
            jnp.where((lane >= HALF) & (lane < HD), sine, 0.0),
            jnp.where(lane < HALF, -sine, 0.0),
        ]
    )


def normalize(rows, gain):
    widened = rows.astype(F32)
    factor = lax.rsqrt(jnp.mean(widened * widened, axis=-1, keepdims=True) + EPS)
    return (widened * factor * gain).astype(BF16)


def head_tile(u_ref, rows, index):
    base, place = (index // 4) * 3 * LANES, index % 4
    lane = lax.broadcasted_iota(jnp.int32, (rows.stop - rows.start, LANES), 1)

    def tile(t):
        return u_ref[rows, base + t * LANES : base + (t + 1) * LANES]

    if place == 0:
        return tile(0)
    if place == 1:
        return pltpu.roll(jnp.where(lane >= 96, tile(0), tile(1)), 32, 1)
    if place == 2:
        return pltpu.roll(jnp.where(lane >= 64, tile(1), tile(2)), 64, 1)
    return pltpu.roll(tile(2), 96, 1)


def fetch(sources, refs, offs_ref, block_rows, columns, target, sem):
    for ref, column, first, blocks in sources:
        for b in range(blocks):
            to = pl.ds(pl.multiple_of(offs_ref[first + b], 16), block_rows)
            source = refs[ref].at[pl.ds(b * block_rows, block_rows), pl.ds(column, columns)]
            pltpu.make_async_copy(source, target(to), sem).start()


def fetch_weights(plan, refs, offs_ref, block_rows, w_ref, sem):
    half = w_ref.shape[1] // len(plan)
    for t, sources in enumerate(plan):
        fetch(sources, refs, offs_ref, block_rows, half, lambda rows: w_ref.at[rows, pl.ds(t * half, half)], sem)


def multiply(x, w_ref, u_ref, rows):
    for n in range(w_ref.shape[1] // 256):
        cols = slice(n * 256, (n + 1) * 256)
        u_ref[:rows, cols] = jnp.dot(x, w_ref[:, cols], preferred_element_type=F32)


def store_heads(u_ref, table_ref, heads_ref, first):
    rows = table_ref.shape[1]
    lane = lax.broadcasted_iota(jnp.int32, (rows, LANES), 1)
    for h in range(8):
        u = head_tile(u_ref, slice(0, rows), h)
        if h in (2, 3):
            u = jnp.where(lane < HD, u, 1.0)
        else:
            u = (
                u * table_ref[0]
                + pltpu.roll(u, HALF, 1) * table_ref[1]
                + pltpu.roll(u, LANES - HALF, 1) * table_ref[2]
            )
        heads_ref[h, first : first + rows, :] = u.astype(BF16)


def turn_decode(u, dtable_ref):
    return (
        u * dtable_ref[0]
        + pltpu.roll(u, HALF, 1) * dtable_ref[1]
        + pltpu.roll(u, u.shape[1] - HALF, 1) * dtable_ref[2]
    ).astype(BF16)


def attend(heads_ref, o_ref, block):
    stretch = o_ref.shape[0]
    causal = lax.broadcasted_iota(jnp.int32, (block, block), 1) <= lax.broadcasted_iota(
        jnp.int32, (block, block), 0
    )
    causal = jnp.concatenate([causal, causal], axis=0)
    for j in range(2):
        for i in range(stretch // block):
            rows = slice(i * block, (i + 1) * block)
            seen = (i + 1) * block
            both = heads_ref[4 + 2 * j : 6 + 2 * j, rows, :].reshape(2 * block, LANES)
            scores = lax.dot_general(
                both, heads_ref[j, :seen, :], (((1,), (1,)), ((), ())), preferred_element_type=F32
            )
            last = jnp.where(causal, scores[:, i * block :], NEGATIVE)
            scores = last if i == 0 else jnp.concatenate([scores[:, : i * block], last], axis=1)
            peak = jnp.max(scores, axis=-1, keepdims=True)
            weights = jnp.exp2((scores - peak) * (SCALE * LOG2E)).astype(BF16)
            mixed = jnp.dot(weights, heads_ref[2 + j, :seen, :], preferred_element_type=F32)
            mixed = (mixed / mixed[:, HD : HD + 1]).astype(BF16)
            for parity in range(2):
                lanes = slice((2 * j + parity) * LANES, (2 * j + parity + 1) * LANES)
                o_ref[rows, lanes] = mixed[parity * block : (parity + 1) * block]


def decode(turned, requests, offset, k_ref, v_ref, len_ref, start_ref, part_ref):
    turned = turned.astype(F32)
    extra = turned.shape[0]
    window, span = k_ref.shape[3], k_ref.shape[2]
    two = 2 * HD

    def widen(values):
        sides = [jnp.zeros((extra, offset), F32)] if offset else []
        sides += [values]
        sides += [jnp.zeros((extra, window - two - offset), F32)] if window - two - offset else []
        return jnp.concatenate(sides, axis=1)

    own_k, own_v = widen(turned[:, :two]), widen(turned[:, two : 2 * two])
    queries = []
    for parity in range(2):
        at = 2 * two + parity * HD
        queries.append(
            widen(jnp.concatenate([turned[:, at : at + HD], turned[:, at + two : at + two + HD]], axis=1))
        )

    def here(i, rows):
        lane = lax.broadcasted_iota(jnp.int32, (rows, window), 1)
        return (lane >= offset + i * HD) & (lane < offset + (i + 1) * HD)

    for parity in range(2):
        product = queries[parity] * own_k
        own = jnp.zeros((extra, window), F32)
        for i in range(2):
            mask = here(i, extra)
            own = own + jnp.where(mask, jnp.sum(jnp.where(mask, product, 0.0), axis=-1, keepdims=True), 0.0)
        rows = slice(parity * requests, (parity + 1) * requests)
        part_ref[2, 0, rows, :] = own_v[:requests]
        part_ref[2, 1, rows, :] = own[:requests] * SCALE
        part_ref[2, 2, rows, :] = jnp.ones((requests, window), F32)

    for r in range(requests):
        query = [
            jnp.where(here(i, 1), queries[parity][r : r + 1], 0.0) for parity in range(2) for i in range(2)
        ]
        query = jnp.concatenate(query + [jnp.zeros((4, window), F32)], axis=0).astype(BF16)
        for b in range(2):
            scores = (
                lax.dot_general(query, k_ref[b, r], (((1,), (1,)), ((), ())), preferred_element_type=F32)
                * SCALE
            )
            live = lax.broadcasted_iota(jnp.int32, scores.shape, 1) + start_ref[b] < len_ref[r]
            scores = jnp.where(live, scores, NEGATIVE)
            peak = jnp.max(scores, axis=-1, keepdims=True)
            expanded = jnp.where(live, jnp.exp(scores - peak), 0.0)
            total = jnp.sum(expanded, axis=-1, keepdims=True)
            sums = jnp.dot(expanded.astype(BF16), v_ref[b, r], preferred_element_type=F32)
            for slot, values in enumerate((sums, peak, total)):
                for parity in range(2):
                    row = parity * requests + r
                    part_ref[b, slot, row : row + 1, :] = sum(
                        jnp.where(here(i, 1), values[2 * parity + i : 2 * parity + i + 1], 0.0) for i in range(2)
                    )


def group_kernel(block_rows, plan, norm, offset, stretches, *refs):
    refs = list(refs)

    def take(count=1):
        taken, refs[:count] = refs[:count], []
        return taken

    with_decode = offset is not None
    (offs_ref,) = take()
    if with_decode:
        lane_ref, len_ref, start_ref = take(3)
    w_refs = take(1 + max(source[0] for sources in plan for source in sources))
    x_hbm = take(stretches)
    (table_ref,) = take()
    if with_decode:
        dx_ref, dtable_ref = take(2)
        caches = take(4)
    o_refs = take(stretches)
    if with_decode:
        (part_ref,) = take()
    if norm:
        xn_hbm = take(stretches)
        if with_decode:
            (dxn_ref,) = take()
    x_refs, u_refs, heads_refs = take(stretches), take(stretches), take(stretches)
    (w_ref,) = take()
    if with_decode:
        k_ref, v_ref = take(2)
    if norm:
        (gain_ref,) = take()
    (sem,) = take()
    stretch = table_ref.shape[1]
    main = pl.ds(0, stretch)

    if norm:
        fetch(plan[2], w_refs, offs_ref, block_rows, LANES, lambda rows: gain_ref.at[rows], sem.at[1])
    loads = [pltpu.make_async_copy(x_hbm[n], x_refs[n].at[main], sem.at[2 + n]) for n in range(stretches)]
    loads[0].start()
    fetch_weights(plan[:2], w_refs, offs_ref, block_rows, w_ref, sem.at[0])
    for load in loads[1:]:
        load.start()
    if with_decode:
        window = k_ref.shape[3]
        for n, source in enumerate(caches):
            lane = pl.multiple_of(lane_ref[0], LANES)
            pltpu.make_async_copy(
                source.at[:, :, pl.ds(lane, window)], (k_ref, v_ref)[n % 2].at[n // 2], sem.at[4 + n]
            ).start()
    if norm:
        pltpu.make_async_copy(gain_ref, gain_ref, sem.at[1]).wait()
        pick = (lax.broadcasted_iota(jnp.int32, (8, LANES), 1) == 0).astype(BF16)
        gain = lax.dot_general(pick, gain_ref[...], (((1,), (1,)), ((), ())), preferred_element_type=F32)[0:1]
        if with_decode:
            dxn_ref[...] = normalize(dx_ref[...], gain)
    saves = []
    for n in range(stretches):
        loads[n].wait()
        if norm:
            def body(i, _):
                rows = pl.ds(pl.multiple_of(i * 64, 64), 64)
                x_refs[n][rows, :] = normalize(x_refs[n][rows, :], gain)
                return 0

            lax.fori_loop(0, stretch // 64, body, 0)
            saves.append(pltpu.make_async_copy(x_refs[n].at[main], xn_hbm[n], sem.at[8 + n]))
            saves[-1].start()
        if n == 0:
            pltpu.make_async_copy(w_ref, w_ref, sem.at[0]).wait()
            if with_decode:
                x_refs[0][stretch:, :] = dxn_ref[...] if norm else dx_ref[...]
        multiply(x_refs[n][...], w_ref, u_refs[n], x_refs[n].shape[0])
        store_heads(u_refs[n], table_ref, heads_refs[n], 0)
        if n == 0 and with_decode:
            turned = turn_decode(u_refs[0][stretch:, :], dtable_ref)
            for m, source in enumerate(caches):
                target = (k_ref, v_ref)[m % 2].at[m // 2]
                pltpu.make_async_copy(target, target, sem.at[4 + m]).wait()
            decode(turned, k_ref.shape[1], offset, k_ref, v_ref, len_ref, start_ref, part_ref)
        attend(heads_refs[n], o_refs[n], 256)
    for save in saves:
        save.wait()


def run_group(rows, tables, offs, w_pieces, block_rows, plan, norm=False, decoding=None):
    stretch, depth = rows[0].shape
    stretches = len(rows)
    width = KV * HD
    smem = pl.BlockSpec(memory_space=pltpu.SMEM)
    vmem = pl.BlockSpec(memory_space=pltpu.VMEM)
    hbm = pl.BlockSpec(memory_space=pl.ANY)
    operands, in_specs, offset, extra = [offs], [smem], None, 0
    if decoding:
        offset, lane, cache_len, starts, dx, dtable, caches = decoding
        requests, span = caches[0].shape[:2]
        extra, window = dx.shape[0], 2 * LANES
        operands += [lane, cache_len, starts]
        in_specs += [smem] * 3
    operands += [*w_pieces, *rows, tables]
    in_specs += [hbm] * (len(w_pieces) + stretches) + [vmem]
    out_shape = [jax.ShapeDtypeStruct((stretch, 4 * LANES), BF16)] * stretches
    out_specs = [vmem] * stretches
    if decoding:
        operands += [dx, dtable, *caches]
        in_specs += [vmem] * 2 + [hbm] * 4
        out_shape.append(jax.ShapeDtypeStruct((3, 3, 2 * requests, window), F32))
        out_specs.append(vmem)
    if norm:
        out_shape += [jax.ShapeDtypeStruct((stretch, depth), BF16)] * stretches
        out_specs += [hbm] * stretches
        if decoding:
            out_shape.append(jax.ShapeDtypeStruct((extra, depth), BF16))
            out_specs.append(vmem)
    rows_all = [stretch + (extra if n == 0 else 0) for n in range(stretches)]
    scratch = [pltpu.VMEM((count, depth), BF16) for count in rows_all]
    scratch += [pltpu.VMEM((count, width), F32) for count in rows_all]
    scratch += [pltpu.VMEM((8, stretch, LANES), BF16)] * stretches
    scratch.append(pltpu.VMEM((depth, width), BF16))
    if decoding:
        scratch += [pltpu.VMEM((2, requests, span, window), BF16)] * 2
    if norm:
        scratch.append(pltpu.VMEM((depth, LANES), BF16))
    scratch.append(pltpu.SemaphoreType.DMA((10,)))
    return pl.pallas_call(
        functools.partial(group_kernel, block_rows, plan, norm, offset, stretches),
        in_specs=in_specs,
        out_specs=out_specs,
        out_shape=out_shape,
        scratch_shapes=scratch,
        compiler_params=pltpu.CompilerParams(vmem_limit_bytes=VMEM_BYTES),
        cost_estimate=cost(1),
        name="group",
    )(*operands)


def output_kernel(requests, block_rows, plan, o_plan, core_ref, offs_ref, *rest):
    count = 1 + max(source[0] for sources in plan for source in sources)
    wo_refs = rest[:count]
    o_refs, rest = rest[count : count + len(o_plan)], rest[count + len(o_plan) :]
    parts_ref, other_ref, out_ref, dec_ref, wo_ref, att_ref, w_sem, o_sem = rest
    step = pl.program_id(0)
    stretch = out_ref.shape[0]
    columns = out_ref.shape[1]
    steps = wo_ref.shape[0]
    half = PAD // 2

    @pl.when(step == 0)
    def _():
        me, core = core_ref[0], core_ref[1]
        o_copies = [
            pltpu.make_async_copy(
                source,
                att_ref.at[core if mine else 1 - core, pl.ds(0, stretch), pl.ds(lane, source.shape[1])],
                o_sem.at[n],
            )
            for n, (source, (mine, lane)) in enumerate(zip(o_refs, o_plan))
        ]
        for copy in o_copies:
            copy.start()
        for t, sources in enumerate(plan):
            for ref, column, first, blocks in sources:
                for b in range(blocks):
                    to = pl.multiple_of(offs_ref[first + b], 16)
                    pltpu.make_async_copy(
                        wo_refs[ref].at[pl.ds(b * block_rows, block_rows), pl.ds(column, columns)],
                        wo_ref.at[t, pl.ds(to, block_rows)],
                        w_sem.at[t],
                    ).start()
        for t in range(steps):
            for h in range(H):
                wo_ref[t, h * LANES + HD : (h + 1) * LANES, :] = jnp.zeros((LANES - HD, columns), BF16)
        extra = att_ref.shape[1] - stretch
        att_ref[:, stretch:, :] = jnp.zeros((2, extra, half), BF16)
        chips = parts_ref.shape[0]
        for parts, place in ((parts_ref, core), (other_ref, 1 - core)):
            blocks = [(jnp.bitwise_xor(me // 2, chip), b) for chip in range(chips) for b in range(2)] + [(0, 2)]
            top = parts[0, 2, 1]
            for slot, b in blocks:
                top = jnp.maximum(top, parts[slot, b, 1])
            numerator, denominator = jnp.zeros_like(top), jnp.zeros_like(top)
            for slot, b in blocks:
                rescale = jnp.exp(parts[slot, b, 1] - top)
                numerator = numerator + rescale * parts[slot, b, 0]
                denominator = denominator + rescale * parts[slot, b, 2]
            mix = numerator / jnp.where(denominator > 0.0, denominator, 1.0)
            window = mix.shape[1] // 2
            for parity in range(2):
                rows = mix[parity * requests : (parity + 1) * requests]
                rows = jnp.concatenate([rows, jnp.zeros((extra - requests, mix.shape[1]), F32)], axis=0)
                for g in range(2):
                    for i in range(2):
                        at = g * window + g * (window - 2 * HD) + i * HD
                        to = (4 * g + 2 * i + parity) * LANES
                        att_ref[place, stretch:, to : to + HD] = rows[:, at : at + HD].astype(BF16)
        for copy in o_copies:
            copy.wait()

    for t in range(steps):
        @pl.when(step == t)
        def _():
            whole = wo_ref.at[t, pl.ds(0, H * HD)]
            pltpu.make_async_copy(whole, whole, w_sem.at[t]).wait()

    projected = jnp.dot(att_ref[0], wo_ref[step, :half], preferred_element_type=F32) + jnp.dot(
        att_ref[1], wo_ref[step, half:], preferred_element_type=F32
    )
    out_ref[...] = projected[:stretch].astype(BF16)
    dec_ref[...] = projected[stretch : stretch + requests].astype(BF16)


def output(attended, parts, other_parts, core, offs, wo_pieces, block_rows, plan, requests):
    stretch = attended[0][0].shape[0]
    width = H * HD
    steps, extra = 2, 16
    smem = pl.BlockSpec(memory_space=pltpu.SMEM)
    vmem = pl.BlockSpec(memory_space=pltpu.VMEM)
    hbm = pl.BlockSpec(memory_space=pl.ANY)
    return pl.pallas_call(
        functools.partial(output_kernel, requests, block_rows, plan, [piece[1:] for piece in attended]),
        grid=(steps,),
        in_specs=[smem] * 2 + [hbm] * (len(wo_pieces) + len(attended)) + [vmem] * 2,
        out_specs=[
            pl.BlockSpec((stretch, width // steps), lambda t: (0, t)),
            pl.BlockSpec((requests, width // steps), lambda t: (0, t)),
        ],
        out_shape=[
            jax.ShapeDtypeStruct((stretch, width), BF16),
            jax.ShapeDtypeStruct((requests, width), BF16),
        ],
        scratch_shapes=[
            pltpu.VMEM((steps, PAD, width // steps), BF16),
            pltpu.VMEM((2, stretch + extra, PAD // 2), BF16),
            pltpu.SemaphoreType.DMA((steps,)),
            pltpu.SemaphoreType.DMA((len(attended),)),
        ],
        compiler_params=pltpu.CompilerParams(
            dimension_semantics=("arbitrary",), vmem_limit_bytes=VMEM_BYTES
        ),
        cost_estimate=cost(1),
        name="output",
    )(core, offs, *wo_pieces, *[piece[0] for piece in attended], parts, other_parts)


def swap(array, mask, n_shard):
    return lax.ppermute(array, "shard", [(i, i ^ mask) for i in range(n_shard)])


def after(array, *others):
    return lax.optimization_barrier((array, *others))[0]


def fence_kernel(operand_ref, token_ref):
    token_ref[...] = jnp.zeros_like(token_ref)


def fence(array):
    token = pl.pallas_call(
        fence_kernel,
        in_specs=[pl.BlockSpec(memory_space=pl.ANY)],
        out_specs=pl.BlockSpec(memory_space=pltpu.VMEM),
        out_shape=jax.ShapeDtypeStruct((1, 1), BF16),
        cost_estimate=cost(200),
        name="fence",
    )(array)
    return token.reshape(())


def along_dp(local, n_dp):
    found = [local]
    for shift in range(1, n_dp):
        found.append(lax.ppermute(local, "dp", [((i + shift) % n_dp, i) for i in range(n_dp)]))
    return found


def pieces_of(here, beside, above, cut, n_shard):
    whole = here.shape[1]
    left, right = swap(beside[:, :cut], 4, n_shard), swap(above[:, cut:], 2, n_shard)
    return [(here, 0, 0, whole), (beside, 1, 0, whole), (above, 2, 0, whole), (left, 3, 0, cut), (right, 3, cut, whole)]


def lay_out(pieces, starts, n_dp, first=0):
    plan = [[] for _ in starts]
    for index, (_, mask, left, right) in enumerate(pieces):
        for column, t in starts.items():
            if left <= column < right:
                plan[t].append((index, column - left, mask * n_dp, n_dp))
    return plan


def group_columns(wqkv, core, width):
    quarter = width // 4
    found = []
    for g in range(2):
        at = (2 * core + g) * quarter
        found += [
            wqkv[:, 2 * width + at : 2 * width + at + quarter],
            wqkv[:, 3 * width + at : 3 * width + at + quarter],
            wqkv[:, 2 * at : 2 * at + 2 * quarter],
        ]
    return jnp.concatenate(found, axis=1)


def per_device(n_dp, n_shard, prefill_x, decode_x, norm_gain, wqkv, wo, k_cache, v_cache, cache_len):
    stretch = prefill_x.shape[0]
    requests, span, width = k_cache.shape
    half = width // 2
    me, me_dp = lax.axis_index("shard"), lax.axis_index("dp")
    core = me % 2
    everyone = ("dp", "shard")
    block_rows = wqkv.shape[0]
    low, high = group_columns(wqkv, 0, width), group_columns(wqkv, 1, width)
    gain_columns = jnp.broadcast_to(norm_gain[:, None], (block_rows, LANES))
    head = LANES + width
    split = n_shard == 8 and block_rows == HALF

    wo_plan = [[(0, 0, 0, H)], [(0, width, 0, H)]]
    wo_offs = jnp.arange(H, dtype=jnp.int32) * LANES
    extra = 16
    dx = jnp.pad(decode_x, ((0, extra - requests), (0, 0)))
    decode_positions = jnp.concatenate([cache_len, jnp.zeros((extra - requests,), jnp.int32)])
    tables = rope_tables(jnp.arange(stretch, dtype=jnp.int32), LANES)
    turning = rope_tables(decode_positions, half)
    quarter = half // 2
    plain = jnp.stack([jnp.ones((extra, quarter), F32)] + [jnp.zeros((extra, quarter), F32)] * 2)
    dtable = jnp.concatenate([turning[:, :, :quarter], plain, turning], axis=2)
    if split:
        first = core == 0
        mine = jnp.concatenate([gain_columns, jnp.where(first, low, high)], axis=1)
        theirs = jnp.concatenate([gain_columns, jnp.where(first, high, low)], axis=1)
        theirs = swap(theirs, 1, n_shard)
        pair = jnp.concatenate([jnp.where(first, mine, theirs), jnp.where(first, theirs, mine)], axis=0)
        order = jnp.arange(n_shard // 2 * n_dp, dtype=jnp.int32)
        chip = (me_dp + order % n_dp) % n_dp * (n_shard // 2) + (me // 2 ^ (order // n_dp))
        block_rows = 2 * block_rows
        offs = chip * block_rows
        sib_x, sib_k, sib_v = [swap(after(array, theirs), 1, n_shard) for array in (prefill_x, k_cache, v_cache)]
        here = jnp.concatenate(along_dp(pair[:, :head], n_dp), axis=0)
        here = after(here, sib_x, sib_k, sib_v, tables, dtable, dx)
        beside, above = swap(here, 2, n_shard), swap(here, 4, n_shard)
        wo = after(wo, here)
        later = after(pair[:, head:], here)
        found = along_dp(later, n_dp)
        later_here = jnp.concatenate(found, axis=0) + fence(later)
        pieces = pieces_of(here, after(beside, later_here), after(above, later_here), LANES + half, n_shard)
        plan = lay_out(pieces, {LANES: 0, LANES + half: 1, 0: 2}, n_dp)
        pieces = [piece[0] for piece in pieces]
        later_here = after(later_here, *pieces)
        beside, above = swap(later_here, 2, n_shard), swap(later_here, 4, n_shard)
    else:
        sib_x, sib_k, sib_v = [swap(array, 1, n_shard) for array in (prefill_x, k_cache, v_cache)]
        offs = jnp.zeros((1,), jnp.int32)
        every = lax.all_gather(jnp.concatenate([gain_columns, low, high], axis=1), everyone, axis=0, tiled=True)
        block_rows = every.shape[0]
        chosen = jnp.where(core == 0, every[:, LANES : LANES + 2 * width], every[:, LANES + 2 * width :])
        pieces = [jnp.concatenate([every[:, :LANES], chosen[:, :width]], axis=1)]
        plan = [[(0, LANES, 0, 1)], [(0, LANES + half, 0, 1)], [(0, 0, 0, 1)]]

    wo_all = lax.all_gather(wo, everyone, axis=0, tiled=True)
    lane = core.astype(jnp.int32).reshape(1) * half
    starts = jnp.stack([me * span, (me ^ 1) * span]).astype(jnp.int32)
    caches = [k_cache, v_cache, sib_k, sib_v]
    sib_o, part, sib_xn, dxn = run_group(
        [sib_x], tables, offs, pieces, block_rows, plan, norm=True,
        decoding=(0, lane, cache_len, starts, dx, dtable, caches),
    )
    later_pieces, later_plan = [], [[(0, 0, 0, 1)], [(0, half, 0, 1)]]
    if split:
        later_pieces = pieces_of(later_here, after(beside, sib_o), after(above, sib_o), half, n_shard)
        later_plan = lay_out(later_pieces, {0: 0, half: 1}, n_dp)
        later_pieces = [piece[0] for piece in later_pieces]
    else:
        later_pieces = [chosen[:, width:]]
    own_o, xn = run_group([after(prefill_x, sib_o)], tables, offs, pieces, block_rows, plan, norm=True)
    mine, theirs = [own_o], [sib_o]
    pieces, plan = [after(later_pieces[0], own_o)] + later_pieces[1:], later_plan
    sib_o, later_part = run_group(
        [sib_xn], tables, offs, pieces, block_rows, plan,
        decoding=(LANES // 2, lane + LANES, cache_len, starts, dxn, dtable, caches),
    )
    theirs.append(sib_o)
    part = jnp.concatenate([part, later_part], axis=-1)
    parts = jnp.stack([part] + [swap(part, 2 * chip, n_shard) for chip in range(1, n_shard // 2)])
    mine += run_group([after(xn, sib_o)], tables, offs, pieces, block_rows, plan)
    other_parts = swap(after(parts, mine[1]), 1, n_shard)
    group_lanes = PAD // 4
    attended = [(piece, True, g * group_lanes) for g, piece in enumerate(mine)]
    attended += [(swap(piece, 1, n_shard), False, g * group_lanes) for g, piece in enumerate(theirs)]
    me_and_core = jnp.stack([me, core]).astype(jnp.int32)
    return output(attended, parts, other_parts, me_and_core, wo_offs, [wo_all], HD, wo_plan, requests)


def solution(mesh):
    in_specs = (
        P(("dp", "shard"), None),
        P("dp", None),
        P(("dp", "shard")),
        P(("dp", "shard"), None),
        P(("dp", "shard"), None),
        P("dp", "shard", None),
        P("dp", "shard", None),
        P("dp"),
    )
    out_specs = (P(("dp", "shard"), None), P("dp", None))
    return jax.shard_map(
        functools.partial(per_device, mesh.shape["dp"], mesh.shape["shard"]),
        mesh=mesh, in_specs=in_specs, out_specs=out_specs, check_vma=False,
    )
```

```python
import functools

import jax
import jax.numpy as jnp
from jax import lax
from jax.experimental import pallas as pl
from jax.experimental.pallas import tpu as pltpu
from jax.sharding import PartitionSpec as P

H = 16
KV = 8
HD = 96
HALF = HD // 2
LANES = 128
PAD = H * LANES

THETA = 100000.0
EPS = 1e-05
NEGATIVE = -1e30
SCALE = HD ** (-0.5)
LOG2E = 1.4426950408889634

BF16 = jnp.bfloat16
F32 = jnp.float32
VMEM_BYTES = 56 * 1024 * 1024


def cost(microseconds):
    return pl.CostEstimate(flops=int(microseconds * 1.1e9), bytes_accessed=100_000, transcendentals=0)


def rope_tables(positions, width, zero):
    lane = jnp.arange(width, dtype=jnp.int32) + zero
    lane = lane % HD if width % HD == 0 else lane
    frequency = jnp.power(THETA, -(lane % HALF).astype(F32) * (2.0 / HD))
    angles = positions.astype(F32)[:, None] * frequency[None, :]
    cosine, sine = jnp.cos(angles), jnp.sin(angles)
    lane = lane[None, :]
    return jnp.stack(
        [
            jnp.where(lane < HD, cosine, 0.0),
            jnp.where((lane >= HALF) & (lane < HD), sine, 0.0),
            jnp.where(lane < HALF, -sine, 0.0),
        ]
    )


def normalize(rows, gain):
    widened = rows.astype(F32)
    factor = lax.rsqrt(jnp.mean(widened * widened, axis=-1, keepdims=True) + EPS)
    return (widened * factor * gain).astype(BF16)


def head_tile(u_ref, rows, index):
    base, place = (index // 4) * 3 * LANES, index % 4
    lane = lax.broadcasted_iota(jnp.int32, (rows.stop - rows.start, LANES), 1)

    def tile(t):
        return u_ref[rows, base + t * LANES : base + (t + 1) * LANES]

    if place == 0:
        return tile(0)
    if place == 1:
        return pltpu.roll(jnp.where(lane >= 96, tile(0), tile(1)), 32, 1)
    if place == 2:
        return pltpu.roll(jnp.where(lane >= 64, tile(1), tile(2)), 64, 1)
    return pltpu.roll(tile(2), 96, 1)


def fetch(sources, refs, offs_ref, block_rows, columns, target, sem):
    for ref, column, first, blocks in sources:
        for b in range(blocks):
            to = pl.ds(pl.multiple_of(offs_ref[first + b], 16), block_rows)
            source = refs[ref].at[pl.ds(b * block_rows, block_rows), pl.ds(column, columns)]
            pltpu.make_async_copy(source, target(to), sem).start()


def fetch_weights(plan, refs, offs_ref, block_rows, w_ref, sem):
    half = w_ref.shape[1] // 2
    joined = [
        source for source in plan[0] if (source[0], source[1] + half, source[2], source[3]) in plan[1]
    ]
    fetch(joined, refs, offs_ref, block_rows, 2 * half, lambda rows: w_ref.at[rows, pl.ds(0, 2 * half)], sem)
    taken = {(ref, first) for ref, _, first, _ in joined}
    for t in range(2):
        single = [source for source in plan[t] if (source[0], source[2]) not in taken]
        fetch(single, refs, offs_ref, block_rows, half, lambda rows: w_ref.at[rows, pl.ds(t * half, half)], sem)


def project(x, w_ref, u_ref, table_ref, heads_ref):
    stretch = table_ref.shape[1]
    lane = lax.broadcasted_iota(jnp.int32, (stretch, LANES), 1)

    def multiply(n):
        cols = slice(n * 256, (n + 1) * 256)
        u_ref[: x.shape[0], cols] = jnp.dot(x, w_ref[:, cols], preferred_element_type=F32)

    def store(h):
        u = head_tile(u_ref, slice(0, stretch), h)
        if h in (2, 3):
            u = jnp.where(lane < HD, u, 1.0)
        else:
            u = (
                u * table_ref[0]
                + pltpu.roll(u, HALF, 1) * table_ref[1]
                + pltpu.roll(u, LANES - HALF, 1) * table_ref[2]
            )
        heads_ref[h] = u.astype(BF16)

    multiply(0)
    multiply(1)
    store(0)
    store(1)
    multiply(2)
    for h in range(2, 8):
        store(h)


def turn_decode(u, dtable_ref):
    return (
        u * dtable_ref[0]
        + pltpu.roll(u, HALF, 1) * dtable_ref[1]
        + pltpu.roll(u, u.shape[1] - HALF, 1) * dtable_ref[2]
    ).astype(BF16)


def attend(heads_ref, o_ref, block):
    stretch = o_ref.shape[0]
    causal = lax.broadcasted_iota(jnp.int32, (block, block), 1) <= lax.broadcasted_iota(
        jnp.int32, (block, block), 0
    )
    causal = jnp.concatenate([causal, causal], axis=0)
    units = [(j, i) for i in range(stretch // block) for j in range(2)]

    def score(j, i):
        both = heads_ref[4 + 2 * j : 6 + 2 * j, i * block : (i + 1) * block, :].reshape(2 * block, LANES)
        return lax.dot_general(
            both, heads_ref[j, : (i + 1) * block, :], (((1,), (1,)), ((), ())), preferred_element_type=F32
        )

    following = score(*units[0])
    for n, (j, i) in enumerate(units):
        scores = following
        if n + 1 < len(units):
            following = score(*units[n + 1])
        last = jnp.where(causal, scores[:, i * block :], NEGATIVE)
        scores = last if i == 0 else jnp.concatenate([scores[:, : i * block], last], axis=1)
        peak = jnp.max(scores, axis=-1, keepdims=True)
        weights = jnp.exp2((scores - peak) * (SCALE * LOG2E)).astype(BF16)
        mixed = jnp.dot(weights, heads_ref[2 + j, : (i + 1) * block, :], preferred_element_type=F32)
        mixed = (mixed / mixed[:, HD : HD + 1]).astype(BF16)
        for parity in range(2):
            lanes = slice((2 * j + parity) * LANES, (2 * j + parity + 1) * LANES)
            o_ref[i * block : (i + 1) * block, lanes] = mixed[parity * block : (parity + 1) * block]


def decode(turned, requests, offset, k_ref, v_ref, len_ref, start_ref, part_ref):
    turned = turned.astype(F32)
    extra = turned.shape[0]
    window, span = k_ref.shape[3], k_ref.shape[2]
    two = 2 * HD

    def widen(values):
        sides = [jnp.zeros((extra, offset), F32)] if offset else []
        sides += [values]
        sides += [jnp.zeros((extra, window - two - offset), F32)] if window - two - offset else []
        return jnp.concatenate(sides, axis=1)

    own_k, own_v = widen(turned[:, :two]), widen(turned[:, two : 2 * two])
    queries = []
    for parity in range(2):
        at = 2 * two + parity * HD
        queries.append(
            widen(jnp.concatenate([turned[:, at : at + HD], turned[:, at + two : at + two + HD]], axis=1))
        )

    def here(i, rows):
        lane = lax.broadcasted_iota(jnp.int32, (rows, window), 1)
        return (lane >= offset + i * HD) & (lane < offset + (i + 1) * HD)

    for parity in range(2):
        product = queries[parity] * own_k
        own = jnp.zeros((extra, window), F32)
        for i in range(2):
            mask = here(i, extra)
            own = own + jnp.where(mask, jnp.sum(jnp.where(mask, product, 0.0), axis=-1, keepdims=True), 0.0)
        rows = slice(parity * requests, (parity + 1) * requests)
        part_ref[2, 0, rows, :] = own_v[:requests]
        part_ref[2, 1, rows, :] = own[:requests] * SCALE
        part_ref[2, 2, rows, :] = jnp.ones((requests, window), F32)

    for r in range(requests):
        query = [
            jnp.where(here(i, 1), queries[parity][r : r + 1], 0.0) for parity in range(2) for i in range(2)
        ]
        query = jnp.concatenate(query + [jnp.zeros((4, window), F32)], axis=0).astype(BF16)
        for b in range(2):
            scores = (
                lax.dot_general(query, k_ref[b, r], (((1,), (1,)), ((), ())), preferred_element_type=F32)
                * SCALE
            )
            start = start_ref[0]
            if b == 1:
                start = start + span - 2 * span * lax.rem(lax.div(start, span), 2)
            live = lax.broadcasted_iota(jnp.int32, scores.shape, 1) + start < len_ref[r]
            scores = jnp.where(live, scores, NEGATIVE)
            peak = jnp.max(scores, axis=-1, keepdims=True)
            expanded = jnp.where(live, jnp.exp(scores - peak), 0.0)
            total = jnp.sum(expanded, axis=-1, keepdims=True)
            sums = jnp.dot(expanded.astype(BF16), v_ref[b, r], preferred_element_type=F32)
            for slot, values in enumerate((sums, peak, total)):
                for parity in range(2):
                    row = parity * requests + r
                    part_ref[b, slot, row : row + 1, :] = sum(
                        jnp.where(here(i, 1), values[2 * parity + i : 2 * parity + i + 1], 0.0) for i in range(2)
                    )


def group_kernel(block_rows, plan, norm, offset, stretches, *refs):
    refs = list(refs)

    def take(count=1):
        taken, refs[:count] = refs[:count], []
        return taken

    with_decode = offset is not None
    (offs_ref,) = take()
    if with_decode:
        lane_ref, len_ref, start_ref = take(3)
    w_refs = take(1 + max(source[0] for sources in plan for source in sources))
    x_hbm = take(stretches)
    (table_ref,) = take()
    if with_decode:
        dx_ref, dtable_ref = take(2)
        (earlier_ref,) = take() if offset else (None,)
        caches = take(4)
    o_refs = take(stretches)
    if with_decode:
        (part_ref,) = take()
    if norm:
        xn_hbm = take(stretches)
        if with_decode:
            (dxn_ref,) = take()
    x_refs, u_refs, heads_refs = take(stretches), take(stretches), take(stretches)
    (w_ref,) = take()
    if with_decode:
        k_ref, v_ref = take(2)
    if norm:
        (gain_ref,) = take()
    (sem,) = take()
    stretch = table_ref.shape[1]
    main = pl.ds(0, stretch)

    if norm:
        fetch(plan[2], w_refs, offs_ref, block_rows, LANES, lambda rows: gain_ref.at[rows], sem.at[1])
    loads = [pltpu.make_async_copy(x_hbm[n], x_refs[n].at[main], sem.at[2 + n]) for n in range(stretches)]
    loads[0].start()
    fetch_weights(plan[:2], w_refs, offs_ref, block_rows, w_ref, sem.at[0])
    for load in loads[1:]:
        load.start()
    if with_decode:
        window = k_ref.shape[3]
        for n, source in enumerate(caches):
            lane = pl.multiple_of(lane_ref[0], LANES)
            pltpu.make_async_copy(
                source.at[:, :, pl.ds(lane, window)], (k_ref, v_ref)[n % 2].at[n // 2], sem.at[4 + n]
            ).start()
    if norm:
        pltpu.make_async_copy(gain_ref, gain_ref, sem.at[1]).wait()
        pick = (lax.broadcasted_iota(jnp.int32, (8, LANES), 1) == 0).astype(BF16)
        gain = lax.dot_general(pick, gain_ref[...], (((1,), (1,)), ((), ())), preferred_element_type=F32)[0:1]
        if with_decode:
            dxn_ref[...] = normalize(dx_ref[...], gain)
    saves = []
    for n in range(stretches):
        loads[n].wait()
        if norm:
            def body(i, _):
                rows = pl.ds(pl.multiple_of(i * 64, 64), 64)
                x_refs[n][rows, :] = normalize(x_refs[n][rows, :], gain)
                return 0

            lax.fori_loop(0, stretch // 64, body, 0, unroll=4)
            saves.append(pltpu.make_async_copy(x_refs[n].at[main], xn_hbm[n], sem.at[8 + n]))
            saves[-1].start()
        if n == 0:
            pltpu.make_async_copy(w_ref, w_ref, sem.at[0]).wait()
            if with_decode:
                x_refs[0][stretch:, :] = dxn_ref[...] if norm else dx_ref[...]
        project(x_refs[n][...], w_ref, u_refs[n], table_ref, heads_refs[n])
        if n == 0 and with_decode:
            turned = turn_decode(u_refs[0][stretch:, :], dtable_ref)
            for m, source in enumerate(caches):
                target = (k_ref, v_ref)[m % 2].at[m // 2]
                pltpu.make_async_copy(target, target, sem.at[4 + m]).wait()
            if offset:
                part_ref[:, :, :, :window] = earlier_ref[...]
            own_lanes = pl.ds(window if offset else 0, window)
            decode(
                turned, k_ref.shape[1], offset, k_ref, v_ref, len_ref, start_ref,
                part_ref.at[:, :, :, own_lanes] if offset else part_ref,
            )
        attend(heads_refs[n], o_refs[n], 256)
    for save in saves:
        save.wait()


def run_group(rows, tables, offs, w_pieces, block_rows, plan, norm=False, decoding=None):
    stretch, depth = rows[0].shape
    stretches = len(rows)
    width = KV * HD
    smem = pl.BlockSpec(memory_space=pltpu.SMEM)
    vmem = pl.BlockSpec(memory_space=pltpu.VMEM)
    hbm = pl.BlockSpec(memory_space=pl.ANY)
    operands, in_specs, offset, extra = [offs], [smem], None, 0
    if decoding:
        offset, lane, cache_len, starts, dx, dtable, earlier, caches = decoding
        requests, span = caches[0].shape[:2]
        extra, window = dx.shape[0], 2 * LANES
        operands += [lane, cache_len, starts]
        in_specs += [smem] * 3
    operands += [*w_pieces, *rows, tables]
    in_specs += [hbm] * (len(w_pieces) + stretches) + [vmem]
    out_shape = [jax.ShapeDtypeStruct((stretch, 4 * LANES), BF16)] * stretches
    out_specs = [vmem] * stretches
    if decoding:
        operands += [dx, dtable, *earlier, *caches]
        in_specs += [vmem] * (2 + len(earlier)) + [hbm] * 4
        out_shape.append(jax.ShapeDtypeStruct((3, 3, 2 * requests, window * (1 + len(earlier))), F32))
        out_specs.append(vmem)
    if norm:
        out_shape += [jax.ShapeDtypeStruct((stretch, depth), BF16)] * stretches
        out_specs += [hbm] * stretches
        if decoding:
            out_shape.append(jax.ShapeDtypeStruct((extra, depth), BF16))
            out_specs.append(vmem)
    rows_all = [stretch + (extra if n == 0 else 0) for n in range(stretches)]
    scratch = [pltpu.VMEM((count, depth), BF16) for count in rows_all]
    scratch += [pltpu.VMEM((count, width), F32) for count in rows_all]
    scratch += [pltpu.VMEM((8, stretch, LANES), BF16)] * stretches
    scratch.append(pltpu.VMEM((depth, width), BF16))
    if decoding:
        scratch += [pltpu.VMEM((2, requests, span, window), BF16)] * 2
    if norm:
        scratch.append(pltpu.VMEM((depth, LANES), BF16))
    scratch.append(pltpu.SemaphoreType.DMA((10,)))
    return pl.pallas_call(
        functools.partial(group_kernel, block_rows, plan, norm, offset, stretches),
        in_specs=in_specs,
        out_specs=out_specs,
        out_shape=out_shape,
        scratch_shapes=scratch,
        compiler_params=pltpu.CompilerParams(vmem_limit_bytes=VMEM_BYTES),
        cost_estimate=cost(1),
        name="group",
    )(*operands)


def output_kernel(requests, block_rows, plan, o_plan, core_ref, *rest):
    count = 1 + max(source[0] for sources in plan for source in sources)
    wo_refs = rest[:count]
    o_refs, rest = rest[count : count + len(o_plan)], rest[count + len(o_plan) :]
    parts_ref, other_ref, out_ref, dec_ref, wo_ref, att_ref, w_sem, o_sem = rest
    step = pl.program_id(0)
    stretch = out_ref.shape[0]
    columns = out_ref.shape[1]
    steps = wo_ref.shape[0]
    half = PAD // 2

    @pl.when(step == 0)
    def _():
        me = core_ref[0]
        core = lax.rem(me, 2)
        o_copies = [
            pltpu.make_async_copy(
                source,
                att_ref.at[core if mine else 1 - core, pl.ds(0, stretch), pl.ds(lane, source.shape[1])],
                o_sem.at[n],
            )
            for n, (source, (mine, lane)) in enumerate(zip(o_refs, o_plan))
        ]
        for copy in o_copies:
            copy.start()
        for t, sources in enumerate(plan):
            for ref, column, first, blocks in sources:
                for b in range(blocks):
                    to = (first + b) * LANES
                    pltpu.make_async_copy(
                        wo_refs[ref].at[pl.ds(b * block_rows, block_rows), pl.ds(column, columns)],
                        wo_ref.at[t, pl.ds(to, block_rows)],
                        w_sem.at[t],
                    ).start()
        for t in range(steps):
            for h in range(H):
                wo_ref[t, h * LANES + HD : (h + 1) * LANES, :] = jnp.zeros((LANES - HD, columns), BF16)
        extra = att_ref.shape[1] - stretch
        att_ref[:, stretch:, :] = jnp.zeros((2, extra, half), BF16)
        chips = parts_ref.shape[0]
        for parts, place in ((parts_ref, core), (other_ref, 1 - core)):
            blocks = [(jnp.bitwise_xor(me // 2, chip), b) for chip in range(chips) for b in range(2)] + [(0, 2)]
            top = parts[0, 2, 1]
            for slot, b in blocks:
                top = jnp.maximum(top, parts[slot, b, 1])
            numerator, denominator = jnp.zeros_like(top), jnp.zeros_like(top)
            for slot, b in blocks:
                rescale = jnp.exp(parts[slot, b, 1] - top)
                numerator = numerator + rescale * parts[slot, b, 0]
                denominator = denominator + rescale * parts[slot, b, 2]
            mix = numerator / jnp.where(denominator > 0.0, denominator, 1.0)
            window = mix.shape[1] // 2
            for parity in range(2):
                rows = mix[parity * requests : (parity + 1) * requests]
                rows = jnp.concatenate([rows, jnp.zeros((extra - requests, mix.shape[1]), F32)], axis=0)
                for g in range(2):
                    for i in range(2):
                        at = g * window + g * (window - 2 * HD) + i * HD
                        to = (4 * g + 2 * i + parity) * LANES
                        att_ref[place, stretch:, to : to + HD] = rows[:, at : at + HD].astype(BF16)
        for copy in o_copies:
            copy.wait()

    for t in range(steps):
        @pl.when(step == t)
        def _():
            whole = wo_ref.at[t, pl.ds(0, H * HD)]
            pltpu.make_async_copy(whole, whole, w_sem.at[t]).wait()

    projected = jnp.dot(att_ref[0], wo_ref[step, :half], preferred_element_type=F32) + jnp.dot(
        att_ref[1], wo_ref[step, half:], preferred_element_type=F32
    )
    out_ref[...] = projected[:stretch].astype(BF16)
    dec_ref[...] = projected[stretch : stretch + requests].astype(BF16)


def output(attended, parts, other_parts, core, wo_pieces, block_rows, plan, requests):
    stretch = attended[0][0].shape[0]
    width = H * HD
    steps, extra = 2, 16
    smem = pl.BlockSpec(memory_space=pltpu.SMEM)
    vmem = pl.BlockSpec(memory_space=pltpu.VMEM)
    hbm = pl.BlockSpec(memory_space=pl.ANY)
    return pl.pallas_call(
        functools.partial(output_kernel, requests, block_rows, plan, [piece[1:] for piece in attended]),
        grid=(steps,),
        in_specs=[smem] + [hbm] * (len(wo_pieces) + len(attended)) + [vmem] * 2,
        out_specs=[
            pl.BlockSpec((stretch, width // steps), lambda t: (0, t)),
            pl.BlockSpec((requests, width // steps), lambda t: (0, t)),
        ],
        out_shape=[
            jax.ShapeDtypeStruct((stretch, width), BF16),
            jax.ShapeDtypeStruct((requests, width), BF16),
        ],
        scratch_shapes=[
            pltpu.VMEM((steps, PAD, width // steps), BF16),
            pltpu.VMEM((2, stretch + extra, PAD // 2), BF16),
            pltpu.SemaphoreType.DMA((steps,)),
            pltpu.SemaphoreType.DMA((len(attended),)),
        ],
        compiler_params=pltpu.CompilerParams(
            dimension_semantics=("arbitrary",), vmem_limit_bytes=VMEM_BYTES
        ),
        cost_estimate=cost(1),
        name="output",
    )(core, *wo_pieces, *[piece[0] for piece in attended], parts, other_parts)


def swap(array, mask, n_shard):
    return lax.ppermute(array, "shard", [(i, i ^ mask) for i in range(n_shard)])


def after(array, *others):
    return lax.optimization_barrier((array, *others))[0]


def fence_kernel(operand_ref, token_ref):
    token_ref[...] = jnp.zeros_like(token_ref)


def fence(array):
    token = pl.pallas_call(
        fence_kernel,
        in_specs=[pl.BlockSpec(memory_space=pl.ANY)],
        out_specs=pl.BlockSpec(memory_space=pltpu.VMEM),
        out_shape=jax.ShapeDtypeStruct((1, 1), BF16),
        cost_estimate=cost(200),
        name="fence",
    )(array)
    return token.reshape(())


def along_dp(local, n_dp):
    found = [local]
    for shift in range(1, n_dp):
        found.append(lax.ppermute(local, "dp", [((i + shift) % n_dp, i) for i in range(n_dp)]))
    return found


def pieces_of(here, beside, above, cut, n_shard):
    whole = here.shape[1]
    left, right = swap(beside[:, :cut], 4, n_shard), swap(above[:, cut:], 2, n_shard)
    return [(here, 0, 0, whole), (beside, 1, 0, whole), (above, 2, 0, whole), (left, 3, 0, cut), (right, 3, cut, whole)]


def lay_out(pieces, starts, n_dp, first=0):
    plan = [[] for _ in starts]
    for index, (_, mask, left, right) in enumerate(pieces):
        for column, t in starts.items():
            if left <= column < right:
                plan[t].append((index, column - left, mask * n_dp, n_dp))
    return plan


def group_columns(wqkv, core, width):
    quarter = width // 4
    found = []
    for g in range(2):
        at = (2 * core + g) * quarter
        found += [
            wqkv[:, 2 * width + at : 2 * width + at + quarter],
            wqkv[:, 3 * width + at : 3 * width + at + quarter],
            wqkv[:, 2 * at : 2 * at + 2 * quarter],
        ]
    return jnp.concatenate(found, axis=1)


def per_device(n_dp, n_shard, prefill_x, decode_x, norm_gain, wqkv, wo, k_cache, v_cache, cache_len):
    stretch = prefill_x.shape[0]
    requests, span, width = k_cache.shape
    half = width // 2
    me, me_dp = lax.axis_index("shard"), lax.axis_index("dp")
    core = me % 2
    everyone = ("dp", "shard")
    block_rows = wqkv.shape[0]
    low, high = group_columns(wqkv, 0, width), group_columns(wqkv, 1, width)
    gain_columns = jnp.broadcast_to(norm_gain[:, None], (block_rows, LANES))
    head = LANES + width
    split = n_shard == 8 and block_rows == HALF

    wo_plan = [[(0, 0, 0, H)], [(0, width, 0, H)]]
    extra = 16
    quarter = half // 2

    def pad_decode(rows):
        return jnp.pad(rows, ((0, extra - requests), (0, 0)))

    def make_tables(lengths):
        decode_positions = jnp.concatenate([lengths, jnp.zeros((extra - requests,), jnp.int32)])
        zero = jnp.minimum(lengths[0], 0)
        turning = rope_tables(decode_positions, half, zero)
        plain = jnp.stack([jnp.ones((extra, quarter), F32)] + [jnp.zeros((extra, quarter), F32)] * 2)
        dtable = jnp.concatenate([turning[:, :, :quarter], plain, turning], axis=2)
        return rope_tables(jnp.arange(stretch, dtype=jnp.int32) + zero, LANES, zero), dtable

    if split:
        first = core == 0
        mine = jnp.concatenate([gain_columns, jnp.where(first, low, high)], axis=1)
        theirs = jnp.concatenate([gain_columns, jnp.where(first, high, low)], axis=1)
        theirs = swap(theirs, 1, n_shard)
        pair = jnp.concatenate([jnp.where(first, mine, theirs), jnp.where(first, theirs, mine)], axis=0)
        order = jnp.arange(n_shard // 2 * n_dp, dtype=jnp.int32)
        chip = (me_dp + order % n_dp) % n_dp * (n_shard // 2) + (me // 2 ^ (order // n_dp))
        block_rows = 2 * block_rows
        offs = chip * block_rows
        sib_x, sib_k, sib_v = [swap(after(array, theirs), 1, n_shard) for array in (prefill_x, k_cache, v_cache)]
        found = along_dp(pair[:, :head], n_dp)
        dx = pad_decode(after(decode_x, found[1]))
        tables, dtable = make_tables(after(cache_len, found[1]))
        found[2:] = [after(block, tables, dtable, dx) for block in found[2:]]
        here = jnp.concatenate(found, axis=0)
        here = after(here, sib_x, sib_k, sib_v, offs)
        beside, above = swap(here, 2, n_shard), swap(here, 4, n_shard)
        wo = after(wo, here)
        later = after(pair[:, head:], here)
        found = along_dp(later, n_dp)
        later_here = jnp.concatenate(found, axis=0) + fence(later)
        pieces = pieces_of(here, after(beside, later_here), after(above, later_here), LANES + half, n_shard)
        plan = lay_out(pieces, {LANES: 0, LANES + half: 1, 0: 2}, n_dp)
        pieces = [piece[0] for piece in pieces]
        later_here = after(later_here, *pieces)
        beside, above = swap(later_here, 2, n_shard), swap(later_here, 4, n_shard)
    else:
        sib_x, sib_k, sib_v = [swap(array, 1, n_shard) for array in (prefill_x, k_cache, v_cache)]
        dx, (tables, dtable) = pad_decode(decode_x), make_tables(cache_len)
        offs = jnp.zeros((1,), jnp.int32)
        every = lax.all_gather(jnp.concatenate([gain_columns, low, high], axis=1), everyone, axis=0, tiled=True)
        block_rows = every.shape[0]
        chosen = jnp.where(core == 0, every[:, LANES : LANES + 2 * width], every[:, LANES + 2 * width :])
        pieces = [jnp.concatenate([every[:, :LANES], chosen[:, :width]], axis=1)]
        plan = [[(0, LANES, 0, 1)], [(0, LANES + half, 0, 1)], [(0, 0, 0, 1)]]

    wo_all = lax.all_gather(wo, everyone, axis=0, tiled=True)
    lane = core.astype(jnp.int32).reshape(1) * half
    starts = (me * span).astype(jnp.int32).reshape(1)
    caches = [k_cache, v_cache, sib_k, sib_v]
    sib_o, part, sib_xn, dxn = run_group(
        [sib_x], tables, offs, pieces, block_rows, plan, norm=True,
        decoding=(0, lane, cache_len, starts, dx, dtable, [], caches),
    )
    later_pieces, later_plan = [], [[(0, 0, 0, 1)], [(0, half, 0, 1)]]
    if split:
        later_pieces = pieces_of(later_here, after(beside, sib_o), after(above, sib_o), half, n_shard)
        later_plan = lay_out(later_pieces, {0: 0, half: 1}, n_dp)
        later_pieces = [piece[0] for piece in later_pieces]
    else:
        later_pieces = [chosen[:, width:]]
    own_o, xn = run_group([after(prefill_x, sib_o)], tables, offs, pieces, block_rows, plan, norm=True)
    mine, theirs = [own_o], [sib_o]
    pieces, plan = [after(later_pieces[0], own_o)] + later_pieces[1:], later_plan
    sib_o, part = run_group(
        [sib_xn], tables, offs, pieces, block_rows, plan,
        decoding=(LANES // 2, lane + LANES, cache_len, starts, dxn, dtable, [part], caches),
    )
    theirs.append(sib_o)
    parts = jnp.stack([part] + [swap(part, 2 * chip, n_shard) for chip in range(1, n_shard // 2)])
    mine += run_group([after(xn, sib_o)], tables, offs, pieces, block_rows, plan)
    other_parts = swap(after(parts, mine[1]), 1, n_shard)
    group_lanes = PAD // 4
    attended = [(piece, True, g * group_lanes) for g, piece in enumerate(mine)]
    attended += [(swap(piece, 1, n_shard), False, g * group_lanes) for g, piece in enumerate(theirs)]
    return output(attended, parts, other_parts, me.astype(jnp.int32).reshape(1), [wo_all], HD, wo_plan, requests)


def solution(mesh):
    in_specs = (
        P(("dp", "shard"), None),
        P("dp", None),
        P(("dp", "shard")),
        P(("dp", "shard"), None),
        P(("dp", "shard"), None),
        P("dp", "shard", None),
        P("dp", "shard", None),
        P("dp"),
    )
    out_specs = (P(("dp", "shard"), None), P("dp", None))
    return jax.shard_map(
        functools.partial(per_device, mesh.shape["dp"], mesh.shape["shard"]),
        mesh=mesh, in_specs=in_specs, out_specs=out_specs, check_vma=False,
    )
```

```python
import functools

import jax
import jax.numpy as jnp
from jax import lax
from jax.experimental import pallas as pl
from jax.experimental.pallas import tpu as pltpu
from jax.sharding import PartitionSpec as P

H = 16
KV = 8
HD = 96
HALF = HD // 2
LANES = 128
PAD = H * LANES

THETA = 100000.0
EPS = 1e-05
NEGATIVE = -1e30
SCALE = HD ** (-0.5)
LOG2E = 1.4426950408889634

BF16 = jnp.bfloat16
F32 = jnp.float32
VMEM_BYTES = 56 * 1024 * 1024


def cost(microseconds):
    return pl.CostEstimate(flops=int(microseconds * 1.1e9), bytes_accessed=100_000, transcendentals=0)


def rope_tables(positions, width, zero):
    lane = jnp.arange(width, dtype=jnp.int32) + zero
    lane = lane % HD if width % HD == 0 else lane
    frequency = jnp.power(THETA, -(lane % HALF).astype(F32) * (2.0 / HD))
    angles = positions.astype(F32)[:, None] * frequency[None, :]
    cosine, sine = jnp.cos(angles), jnp.sin(angles)
    lane = lane[None, :]
    return jnp.stack(
        [
            jnp.where(lane < HD, cosine, 0.0),
            jnp.where((lane >= HALF) & (lane < HD), sine, 0.0),
            jnp.where(lane < HALF, -sine, 0.0),
        ]
    )


def normalize(rows, gain):
    widened = rows.astype(F32)
    factor = lax.rsqrt(jnp.mean(widened * widened, axis=-1, keepdims=True) + EPS)
    return (widened * factor * gain).astype(BF16)


def head_tile(u_ref, rows, index):
    base, place = (index // 4) * 3 * LANES, index % 4
    lane = lax.broadcasted_iota(jnp.int32, (rows.stop - rows.start, LANES), 1)

    def tile(t):
        return u_ref[rows, base + t * LANES : base + (t + 1) * LANES]

    if place == 0:
        return tile(0)
    if place == 1:
        return pltpu.roll(jnp.where(lane >= 96, tile(0), tile(1)), 32, 1)
    if place == 2:
        return pltpu.roll(jnp.where(lane >= 64, tile(1), tile(2)), 64, 1)
    return pltpu.roll(tile(2), 96, 1)


def fetch(sources, refs, offs_ref, block_rows, columns, target, sem):
    for ref, column, first, blocks in sources:
        for b in range(blocks):
            to = pl.ds(pl.multiple_of(offs_ref[first + b], 16), block_rows)
            source = refs[ref].at[pl.ds(b * block_rows, block_rows), pl.ds(column, columns)]
            pltpu.make_async_copy(source, target(to), sem).start()


def fetch_weights(plan, refs, offs_ref, block_rows, w_ref, sem):
    half = w_ref.shape[1] // 2
    joined = [
        source for source in plan[0] if (source[0], source[1] + half, source[2], source[3]) in plan[1]
    ]
    fetch(joined, refs, offs_ref, block_rows, 2 * half, lambda rows: w_ref.at[rows, pl.ds(0, 2 * half)], sem)
    taken = {(ref, first) for ref, _, first, _ in joined}
    for t in range(2):
        single = [source for source in plan[t] if (source[0], source[2]) not in taken]
        fetch(single, refs, offs_ref, block_rows, half, lambda rows: w_ref.at[rows, pl.ds(t * half, half)], sem)


def project(x, w_ref, u_ref, table_ref, heads_ref):
    stretch = table_ref.shape[1]
    lane = lax.broadcasted_iota(jnp.int32, (stretch, LANES), 1)

    def multiply(n):
        cols = slice(n * 256, (n + 1) * 256)
        u_ref[: x.shape[0], cols] = jnp.dot(x, w_ref[:, cols], preferred_element_type=F32)

    def store(h):
        u = head_tile(u_ref, slice(0, stretch), h)
        if h in (2, 3):
            u = jnp.where(lane < HD, u, 1.0)
        else:
            u = (
                u * table_ref[0]
                + pltpu.roll(u, HALF, 1) * table_ref[1]
                + pltpu.roll(u, LANES - HALF, 1) * table_ref[2]
            )
        heads_ref[h] = u.astype(BF16)

    multiply(0)
    multiply(1)
    store(0)
    store(1)
    multiply(2)
    for h in range(2, 8):
        store(h)


def turn_decode(u, dtable_ref):
    return (
        u * dtable_ref[0]
        + pltpu.roll(u, HALF, 1) * dtable_ref[1]
        + pltpu.roll(u, u.shape[1] - HALF, 1) * dtable_ref[2]
    ).astype(BF16)


def attend(heads_ref, o_ref, block):
    stretch = o_ref.shape[0]
    causal = lax.broadcasted_iota(jnp.int32, (block, block), 1) <= lax.broadcasted_iota(
        jnp.int32, (block, block), 0
    )
    causal = jnp.concatenate([causal, causal], axis=0)
    units = [(j, i) for i in range(stretch // block) for j in range(2)]

    def score(j, i):
        both = heads_ref[4 + 2 * j : 6 + 2 * j, i * block : (i + 1) * block, :].reshape(2 * block, LANES)
        return lax.dot_general(
            both, heads_ref[j, : (i + 1) * block, :], (((1,), (1,)), ((), ())), preferred_element_type=F32
        )

    following = score(*units[0])
    for n, (j, i) in enumerate(units):
        scores = following
        if n + 1 < len(units):
            following = score(*units[n + 1])
        last = jnp.where(causal, scores[:, i * block :], NEGATIVE)
        scores = last if i == 0 else jnp.concatenate([scores[:, : i * block], last], axis=1)
        peak = jnp.max(scores, axis=-1, keepdims=True)
        weights = jnp.exp2(scores * (SCALE * LOG2E) - peak * (SCALE * LOG2E)).astype(BF16)
        mixed = jnp.dot(weights, heads_ref[2 + j, : (i + 1) * block, :], preferred_element_type=F32)
        mixed = (mixed / mixed[:, HD : HD + 1]).astype(BF16)
        for parity in range(2):
            lanes = slice((2 * j + parity) * LANES, (2 * j + parity + 1) * LANES)
            o_ref[i * block : (i + 1) * block, lanes] = mixed[parity * block : (parity + 1) * block]


def decode(turned, requests, offset, k_ref, v_ref, len_ref, start_ref, part_ref):
    turned = turned.astype(F32)
    extra = turned.shape[0]
    window, span = k_ref.shape[3], k_ref.shape[2]
    two = 2 * HD

    def widen(values):
        sides = [jnp.zeros((extra, offset), F32)] if offset else []
        sides += [values]
        sides += [jnp.zeros((extra, window - two - offset), F32)] if window - two - offset else []
        return jnp.concatenate(sides, axis=1)

    own_k, own_v = widen(turned[:, :two]), widen(turned[:, two : 2 * two])
    queries = []
    for parity in range(2):
        at = 2 * two + parity * HD
        queries.append(
            widen(jnp.concatenate([turned[:, at : at + HD], turned[:, at + two : at + two + HD]], axis=1))
        )

    def here(i, rows):
        lane = lax.broadcasted_iota(jnp.int32, (rows, window), 1)
        return (lane >= offset + i * HD) & (lane < offset + (i + 1) * HD)

    for parity in range(2):
        product = queries[parity] * own_k
        own = jnp.zeros((extra, window), F32)
        for i in range(2):
            mask = here(i, extra)
            own = own + jnp.where(mask, jnp.sum(jnp.where(mask, product, 0.0), axis=-1, keepdims=True), 0.0)
        rows = slice(parity * requests, (parity + 1) * requests)
        part_ref[2, 0, rows, :] = own_v[:requests]
        part_ref[2, 1, rows, :] = own[:requests] * SCALE
        part_ref[2, 2, rows, :] = jnp.ones((requests, window), F32)

    for r in range(requests):
        query = [
            jnp.where(here(i, 1), queries[parity][r : r + 1], 0.0) for parity in range(2) for i in range(2)
        ]
        query = jnp.concatenate(query + [jnp.zeros((4, window), F32)], axis=0).astype(BF16)
        for b in range(2):
            scores = (
                lax.dot_general(query, k_ref[b, r], (((1,), (1,)), ((), ())), preferred_element_type=F32)
                * SCALE
            )
            start = start_ref[0]
            if b == 1:
                start = start + span - 2 * span * lax.rem(lax.div(start, span), 2)
            live = lax.broadcasted_iota(jnp.int32, scores.shape, 1) + start < len_ref[r]
            scores = jnp.where(live, scores, NEGATIVE)
            peak = jnp.max(scores, axis=-1, keepdims=True)
            expanded = jnp.where(live, jnp.exp(scores - peak), 0.0)
            total = jnp.sum(expanded, axis=-1, keepdims=True)
            sums = jnp.dot(expanded.astype(BF16), v_ref[b, r], preferred_element_type=F32)
            for slot, values in enumerate((sums, peak, total)):
                for parity in range(2):
                    row = parity * requests + r
                    part_ref[b, slot, row : row + 1, :] = sum(
                        jnp.where(here(i, 1), values[2 * parity + i : 2 * parity + i + 1], 0.0) for i in range(2)
                    )


def group_kernel(block_rows, plan, norm, offset, stretches, *refs):
    refs = list(refs)

    def take(count=1):
        taken, refs[:count] = refs[:count], []
        return taken

    with_decode = offset is not None
    (offs_ref,) = take()
    if with_decode:
        lane_ref, len_ref, start_ref = take(3)
    w_refs = take(1 + max(source[0] for sources in plan for source in sources))
    x_hbm = take(stretches)
    (table_ref,) = take()
    if with_decode:
        dx_ref, dtable_ref = take(2)
        (earlier_ref,) = take() if offset else (None,)
        caches = take(4)
    o_refs = take(stretches)
    if with_decode:
        (part_ref,) = take()
    if norm:
        xn_hbm = take(stretches)
        if with_decode:
            (dxn_ref,) = take()
    x_refs, u_refs, heads_refs = take(stretches), take(stretches), take(stretches)
    (w_ref,) = take()
    if with_decode:
        k_ref, v_ref = take(2)
    if norm:
        (gain_ref,) = take()
    (sem,) = take()
    stretch = table_ref.shape[1]
    main = pl.ds(0, stretch)

    if norm:
        fetch(plan[2], w_refs, offs_ref, block_rows, LANES, lambda rows: gain_ref.at[rows], sem.at[1])
    loads = [pltpu.make_async_copy(x_hbm[n], x_refs[n].at[main], sem.at[2 + n]) for n in range(stretches)]
    loads[0].start()
    fetch_weights(plan[:2], w_refs, offs_ref, block_rows, w_ref, sem.at[0])
    for load in loads[1:]:
        load.start()
    if with_decode:
        window = k_ref.shape[3]
        for n, source in enumerate(caches):
            lane = pl.multiple_of(lane_ref[0], LANES)
            pltpu.make_async_copy(
                source.at[:, :, pl.ds(lane, window)], (k_ref, v_ref)[n % 2].at[n // 2], sem.at[4 + n]
            ).start()
    if norm:
        pltpu.make_async_copy(gain_ref, gain_ref, sem.at[1]).wait()
        pick = (lax.broadcasted_iota(jnp.int32, (8, LANES), 1) == 0).astype(BF16)
        gain = lax.dot_general(pick, gain_ref[...], (((1,), (1,)), ((), ())), preferred_element_type=F32)[0:1]
        if with_decode:
            dxn_ref[...] = normalize(dx_ref[...], gain)
    saves = []
    for n in range(stretches):
        loads[n].wait()
        if norm:
            def body(i, _):
                rows = pl.ds(pl.multiple_of(i * 64, 64), 64)
                x_refs[n][rows, :] = normalize(x_refs[n][rows, :], gain)
                return 0

            lax.fori_loop(0, stretch // 64, body, 0, unroll=4)
            saves.append(pltpu.make_async_copy(x_refs[n].at[main], xn_hbm[n], sem.at[8 + n]))
            saves[-1].start()
        if n == 0:
            pltpu.make_async_copy(w_ref, w_ref, sem.at[0]).wait()
            if with_decode:
                x_refs[0][stretch:, :] = dxn_ref[...] if norm else dx_ref[...]
        project(x_refs[n][...], w_ref, u_refs[n], table_ref, heads_refs[n])
        if n == 0 and with_decode:
            turned = turn_decode(u_refs[0][stretch:, :], dtable_ref)
            for m, source in enumerate(caches):
                target = (k_ref, v_ref)[m % 2].at[m // 2]
                pltpu.make_async_copy(target, target, sem.at[4 + m]).wait()
            if offset:
                part_ref[:, :, :, :window] = earlier_ref[...]
            own_lanes = pl.ds(window if offset else 0, window)
            decode(
                turned, k_ref.shape[1], offset, k_ref, v_ref, len_ref, start_ref,
                part_ref.at[:, :, :, own_lanes] if offset else part_ref,
            )
        attend(heads_refs[n], o_refs[n], 256)
    for save in saves:
        save.wait()


def run_group(rows, tables, offs, w_pieces, block_rows, plan, norm=False, decoding=None):
    stretch, depth = rows[0].shape
    stretches = len(rows)
    width = KV * HD
    smem = pl.BlockSpec(memory_space=pltpu.SMEM)
    vmem = pl.BlockSpec(memory_space=pltpu.VMEM)
    hbm = pl.BlockSpec(memory_space=pl.ANY)
    operands, in_specs, offset, extra = [offs], [smem], None, 0
    if decoding:
        offset, lane, cache_len, starts, dx, dtable, earlier, caches = decoding
        requests, span = caches[0].shape[:2]
        extra, window = dx.shape[0], 2 * LANES
        operands += [lane, cache_len, starts]
        in_specs += [smem] * 3
    operands += [*w_pieces, *rows, tables]
    in_specs += [hbm] * (len(w_pieces) + stretches) + [vmem]
    out_shape = [jax.ShapeDtypeStruct((stretch, 4 * LANES), BF16)] * stretches
    out_specs = [vmem] * stretches
    if decoding:
        operands += [dx, dtable, *earlier, *caches]
        in_specs += [vmem] * (2 + len(earlier)) + [hbm] * 4
        out_shape.append(jax.ShapeDtypeStruct((3, 3, 2 * requests, window * (1 + len(earlier))), F32))
        out_specs.append(vmem)
    if norm:
        out_shape += [jax.ShapeDtypeStruct((stretch, depth), BF16)] * stretches
        out_specs += [hbm] * stretches
        if decoding:
            out_shape.append(jax.ShapeDtypeStruct((extra, depth), BF16))
            out_specs.append(vmem)
    rows_all = [stretch + (extra if n == 0 else 0) for n in range(stretches)]
    scratch = [pltpu.VMEM((count, depth), BF16) for count in rows_all]
    scratch += [pltpu.VMEM((count, width), F32) for count in rows_all]
    scratch += [pltpu.VMEM((8, stretch, LANES), BF16)] * stretches
    scratch.append(pltpu.VMEM((depth, width), BF16))
    if decoding:
        scratch += [pltpu.VMEM((2, requests, span, window), BF16)] * 2
    if norm:
        scratch.append(pltpu.VMEM((depth, LANES), BF16))
    scratch.append(pltpu.SemaphoreType.DMA((10,)))
    return pl.pallas_call(
        functools.partial(group_kernel, block_rows, plan, norm, offset, stretches),
        in_specs=in_specs,
        out_specs=out_specs,
        out_shape=out_shape,
        scratch_shapes=scratch,
        compiler_params=pltpu.CompilerParams(vmem_limit_bytes=VMEM_BYTES),
        cost_estimate=cost(1),
        name="group",
    )(*operands)


def output_kernel(requests, block_rows, plan, o_plan, core_ref, *rest):
    count = 1 + max(source[0] for sources in plan for source in sources)
    wo_refs = rest[:count]
    o_refs, rest = rest[count : count + len(o_plan)], rest[count + len(o_plan) :]
    parts_ref, other_ref, out_ref, dec_ref, wo_ref, att_ref, w_sem, o_sem = rest
    step = pl.program_id(0)
    stretch = out_ref.shape[0]
    columns = out_ref.shape[1]
    steps = wo_ref.shape[0]
    half = PAD // 2

    @pl.when(step == 0)
    def _():
        me = core_ref[0]
        core = lax.rem(me, 2)
        o_copies = [
            pltpu.make_async_copy(
                source,
                att_ref.at[core if mine else 1 - core, pl.ds(0, stretch), pl.ds(lane, source.shape[1])],
                o_sem.at[n],
            )
            for n, (source, (mine, lane)) in enumerate(zip(o_refs, o_plan))
        ]
        for copy in o_copies:
            copy.start()
        for t, sources in enumerate(plan):
            for ref, column, first, blocks in sources:
                for b in range(blocks):
                    to = (first + b) * LANES
                    pltpu.make_async_copy(
                        wo_refs[ref].at[pl.ds(b * block_rows, block_rows), pl.ds(column, columns)],
                        wo_ref.at[t, pl.ds(to, block_rows)],
                        w_sem.at[t],
                    ).start()
        for t in range(steps):
            for h in range(H):
                wo_ref[t, h * LANES + HD : (h + 1) * LANES, :] = jnp.zeros((LANES - HD, columns), BF16)
        extra = att_ref.shape[1] - stretch
        att_ref[:, stretch:, :] = jnp.zeros((2, extra, half), BF16)
        chips = parts_ref.shape[0]
        for parts, place in ((parts_ref, core), (other_ref, 1 - core)):
            blocks = [(jnp.bitwise_xor(me // 2, chip), b) for chip in range(chips) for b in range(2)] + [(0, 2)]
            top = parts[0, 2, 1]
            for slot, b in blocks:
                top = jnp.maximum(top, parts[slot, b, 1])
            numerator, denominator = jnp.zeros_like(top), jnp.zeros_like(top)
            for slot, b in blocks:
                rescale = jnp.exp(parts[slot, b, 1] - top)
                numerator = numerator + rescale * parts[slot, b, 0]
                denominator = denominator + rescale * parts[slot, b, 2]
            mix = numerator / jnp.where(denominator > 0.0, denominator, 1.0)
            window = mix.shape[1] // 2
            for parity in range(2):
                rows = mix[parity * requests : (parity + 1) * requests]
                rows = jnp.concatenate([rows, jnp.zeros((extra - requests, mix.shape[1]), F32)], axis=0)
                for g in range(2):
                    for i in range(2):
                        at = g * window + g * (window - 2 * HD) + i * HD
                        to = (4 * g + 2 * i + parity) * LANES
                        att_ref[place, stretch:, to : to + HD] = rows[:, at : at + HD].astype(BF16)
        for copy in o_copies:
            copy.wait()

    for t in range(steps):
        @pl.when(step == t)
        def _():
            whole = wo_ref.at[t, pl.ds(0, H * HD)]
            pltpu.make_async_copy(whole, whole, w_sem.at[t]).wait()

    projected = jnp.dot(att_ref[0], wo_ref[step, :half], preferred_element_type=F32) + jnp.dot(
        att_ref[1], wo_ref[step, half:], preferred_element_type=F32
    )
    out_ref[...] = projected[:stretch].astype(BF16)
    dec_ref[...] = projected[stretch : stretch + requests].astype(BF16)


def output(attended, parts, other_parts, core, wo_pieces, block_rows, plan, requests):
    stretch = attended[0][0].shape[0]
    width = H * HD
    steps, extra = 2, 16
    smem = pl.BlockSpec(memory_space=pltpu.SMEM)
    vmem = pl.BlockSpec(memory_space=pltpu.VMEM)
    hbm = pl.BlockSpec(memory_space=pl.ANY)
    return pl.pallas_call(
        functools.partial(output_kernel, requests, block_rows, plan, [piece[1:] for piece in attended]),
        grid=(steps,),
        in_specs=[smem] + [hbm] * (len(wo_pieces) + len(attended)) + [vmem] * 2,
        out_specs=[
            pl.BlockSpec((stretch, width // steps), lambda t: (0, t)),
            pl.BlockSpec((requests, width // steps), lambda t: (0, t)),
        ],
        out_shape=[
            jax.ShapeDtypeStruct((stretch, width), BF16),
            jax.ShapeDtypeStruct((requests, width), BF16),
        ],
        scratch_shapes=[
            pltpu.VMEM((steps, PAD, width // steps), BF16),
            pltpu.VMEM((2, stretch + extra, PAD // 2), BF16),
            pltpu.SemaphoreType.DMA((steps,)),
            pltpu.SemaphoreType.DMA((len(attended),)),
        ],
        compiler_params=pltpu.CompilerParams(
            dimension_semantics=("arbitrary",), vmem_limit_bytes=VMEM_BYTES
        ),
        cost_estimate=cost(1),
        name="output",
    )(core, *wo_pieces, *[piece[0] for piece in attended], parts, other_parts)


def swap(array, mask, n_shard):
    return lax.ppermute(array, "shard", [(i, i ^ mask) for i in range(n_shard)])


def after(array, *others):
    return lax.optimization_barrier((array, *others))[0]


def fence_kernel(operand_ref, token_ref):
    token_ref[...] = jnp.zeros_like(token_ref)


def fence(array):
    token = pl.pallas_call(
        fence_kernel,
        in_specs=[pl.BlockSpec(memory_space=pl.ANY)],
        out_specs=pl.BlockSpec(memory_space=pltpu.VMEM),
        out_shape=jax.ShapeDtypeStruct((1, 1), BF16),
        cost_estimate=cost(200),
        name="fence",
    )(array)
    return token.reshape(())


def along_dp(local, n_dp):
    found = [local]
    for shift in range(1, n_dp):
        found.append(lax.ppermute(local, "dp", [((i + shift) % n_dp, i) for i in range(n_dp)]))
    return found


def pieces_of(here, beside, above, cut, n_shard):
    whole = here.shape[1]
    left, right = swap(beside[:, :cut], 4, n_shard), swap(above[:, cut:], 2, n_shard)
    return [(here, 0, 0, whole), (beside, 1, 0, whole), (above, 2, 0, whole), (left, 3, 0, cut), (right, 3, cut, whole)]


def lay_out(pieces, starts, n_dp, first=0):
    plan = [[] for _ in starts]
    for index, (_, mask, left, right) in enumerate(pieces):
        for column, t in starts.items():
            if left <= column < right:
                plan[t].append((index, column - left, mask * n_dp, n_dp))
    return plan


def group_columns(wqkv, core, width):
    quarter = width // 4
    found = []
    for g in range(2):
        at = (2 * core + g) * quarter
        found += [
            wqkv[:, 2 * width + at : 2 * width + at + quarter],
            wqkv[:, 3 * width + at : 3 * width + at + quarter],
            wqkv[:, 2 * at : 2 * at + 2 * quarter],
        ]
    return jnp.concatenate(found, axis=1)


def per_device(n_dp, n_shard, prefill_x, decode_x, norm_gain, wqkv, wo, k_cache, v_cache, cache_len):
    stretch = prefill_x.shape[0]
    requests, span, width = k_cache.shape
    half = width // 2
    me, me_dp = lax.axis_index("shard"), lax.axis_index("dp")
    core = me % 2
    everyone = ("dp", "shard")
    block_rows = wqkv.shape[0]
    low, high = group_columns(wqkv, 0, width), group_columns(wqkv, 1, width)
    gain_columns = jnp.broadcast_to(norm_gain[:, None], (block_rows, LANES))
    head = LANES + width
    split = n_shard == 8 and block_rows == HALF

    wo_plan = [[(0, 0, 0, H)], [(0, width, 0, H)]]
    extra = 16
    quarter = half // 2

    def pad_decode(rows):
        return jnp.pad(rows, ((0, extra - requests), (0, 0)))

    def make_tables(lengths):
        decode_positions = jnp.concatenate([lengths, jnp.zeros((extra - requests,), jnp.int32)])
        zero = jnp.minimum(lengths[0], 0)
        turning = rope_tables(decode_positions, half, zero)
        plain = jnp.stack([jnp.ones((extra, quarter), F32)] + [jnp.zeros((extra, quarter), F32)] * 2)
        dtable = jnp.concatenate([turning[:, :, :quarter], plain, turning], axis=2)
        return rope_tables(jnp.arange(stretch, dtype=jnp.int32) + zero, LANES, zero), dtable

    if split:
        first = core == 0
        mine = jnp.concatenate([gain_columns, jnp.where(first, low, high)], axis=1)
        theirs = jnp.concatenate([gain_columns, jnp.where(first, high, low)], axis=1)
        theirs = swap(theirs, 1, n_shard)
        pair = jnp.concatenate([jnp.where(first, mine, theirs), jnp.where(first, theirs, mine)], axis=0)
        order = jnp.arange(n_shard // 2 * n_dp, dtype=jnp.int32)
        chip = (me_dp + order % n_dp) % n_dp * (n_shard // 2) + (me // 2 ^ (order // n_dp))
        block_rows = 2 * block_rows
        offs = chip * block_rows
        sib_x, sib_k, sib_v = [swap(after(array, theirs), 1, n_shard) for array in (prefill_x, k_cache, v_cache)]
        found = along_dp(pair[:, :head], n_dp)
        dx = pad_decode(after(decode_x, found[1]))
        tables, dtable = make_tables(after(cache_len, found[1]))
        found[2:] = [after(block, tables, dtable, dx) for block in found[2:]]
        here = jnp.concatenate(found, axis=0)
        here = after(here, offs)
        beside, above = swap(here, 2, n_shard), swap(here, 4, n_shard)
        wo = after(wo, here)
        later = after(pair[:, head:], here, sib_x, sib_k, sib_v)
        found = along_dp(later, n_dp)
        found[1:] = [after(block, beside, above) for block in found[1:]]
        later_here = jnp.concatenate(found, axis=0) + fence(later)
        pieces = pieces_of(here, after(beside, later_here), after(above, later_here), LANES + half, n_shard)
        plan = lay_out(pieces, {LANES: 0, LANES + half: 1, 0: 2}, n_dp)
        pieces = [piece[0] for piece in pieces]
        later_here = after(later_here, *pieces)
        beside, above = swap(later_here, 2, n_shard), swap(later_here, 4, n_shard)
    else:
        sib_x, sib_k, sib_v = [swap(array, 1, n_shard) for array in (prefill_x, k_cache, v_cache)]
        dx, (tables, dtable) = pad_decode(decode_x), make_tables(cache_len)
        offs = jnp.zeros((1,), jnp.int32)
        every = lax.all_gather(jnp.concatenate([gain_columns, low, high], axis=1), everyone, axis=0, tiled=True)
        block_rows = every.shape[0]
        chosen = jnp.where(core == 0, every[:, LANES : LANES + 2 * width], every[:, LANES + 2 * width :])
        pieces = [jnp.concatenate([every[:, :LANES], chosen[:, :width]], axis=1)]
        plan = [[(0, LANES, 0, 1)], [(0, LANES + half, 0, 1)], [(0, 0, 0, 1)]]

    wo_all = lax.all_gather(wo, everyone, axis=0, tiled=True)
    lane = core.astype(jnp.int32).reshape(1) * half
    starts = (me * span).astype(jnp.int32).reshape(1)
    caches = [k_cache, v_cache, sib_k, sib_v]
    sib_o, part, sib_xn, dxn = run_group(
        [sib_x], tables, offs, pieces, block_rows, plan, norm=True,
        decoding=(0, lane, cache_len, starts, dx, dtable, [], caches),
    )
    later_pieces, later_plan = [], [[(0, 0, 0, 1)], [(0, half, 0, 1)]]
    if split:
        later_pieces = pieces_of(later_here, after(beside, sib_o), after(above, sib_o), half, n_shard)
        later_plan = lay_out(later_pieces, {0: 0, half: 1}, n_dp)
        later_pieces = [piece[0] for piece in later_pieces]
    else:
        later_pieces = [chosen[:, width:]]
    own_o, xn = run_group([after(prefill_x, sib_o)], tables, offs, pieces, block_rows, plan, norm=True)
    mine, theirs = [own_o], [sib_o]
    pieces, plan = [after(later_pieces[0], own_o)] + later_pieces[1:], later_plan
    sib_o, part = run_group(
        [sib_xn], tables, offs, pieces, block_rows, plan,
        decoding=(LANES // 2, lane + LANES, cache_len, starts, dxn, dtable, [part], caches),
    )
    theirs.append(sib_o)
    parts = jnp.stack([part] + [swap(part, 2 * chip, n_shard) for chip in range(1, n_shard // 2)])
    mine += run_group([after(xn, sib_o)], tables, offs, pieces, block_rows, plan)
    other_parts = swap(after(parts, mine[1]), 1, n_shard)
    group_lanes = PAD // 4
    attended = [(piece, True, g * group_lanes) for g, piece in enumerate(mine)]
    attended += [(swap(piece, 1, n_shard), False, g * group_lanes) for g, piece in enumerate(theirs)]
    return output(attended, parts, other_parts, me.astype(jnp.int32).reshape(1), [wo_all], HD, wo_plan, requests)


def solution(mesh):
    in_specs = (
        P(("dp", "shard"), None),
        P("dp", None),
        P(("dp", "shard")),
        P(("dp", "shard"), None),
        P(("dp", "shard"), None),
        P("dp", "shard", None),
        P("dp", "shard", None),
        P("dp"),
    )
    out_specs = (P(("dp", "shard"), None), P("dp", None))
    return jax.shard_map(
        functools.partial(per_device, mesh.shape["dp"], mesh.shape["shard"]),
        mesh=mesh, in_specs=in_specs, out_specs=out_specs, check_vma=False,
    )
```
